512 devices in a mesh: gx: 128 (over x, y_hi, z), gy: 2 (over core), gz: 2 (over y_lo).
Axes of the slice: x: 4, y: 4 (y_hi: 2, y_lo: 2; y = y_hi * 2 + y_lo), z: 16, core: 2. Of those that a mesh axis runs over, the one named last changes fastest.
Arguments:
- concentration_levels: float32 [3, 17, 512, 16, 256], P(None, None, 'gx', 'gz', 'gy'), may hold values from 0.0001 to 1
- thermal_levels: float32 [3, 512, 16, 256], P(None, 'gx', 'gz', 'gy'), may hold values from 4 to 6
- fluid_velocity: float32 [3, 512, 16, 256], P(None, 'gx', 'gz', 'gy'), may hold values from -4 to 4
- diffusivity: float32 [18], replicated, may hold values from 0.15 to 0.6
- natural_logged_prefactors: float32 [73], replicated, may hold values from -3 to 0
- energy_barrier_kelvin: float32 [73], replicated, may hold values from 1 to 8
- enthalpy_yield_per_mole: float32 [17], replicated, may hold values from -0.3 to 0.3
- stoichiometric_member_table: int32 [4, 73], replicated, may hold values from 0 to 17
Outputs:
- species_next: float32 [17, 512, 16, 256], P(None, 'gx', 'gz', 'gy')
- temperature_next: float32 [512, 16, 256], P('gx', 'gz', 'gy')
The draws below stay inside these ranges and needn't reach their ends.
Inputs may be any that keep to these rules, and one draw needn't show every extreme that they name: `stoichiometric_member_table`: rows 0 and 1 give each reaction's two reactants and rows 2 and 3 its two products; the value 17 means the collision partner M in rows 0 and 1 and no product in rows 2 and 3.
All inputs are finite; a program needn't handle non-finite values.
Results may differ from the reference program's by a relative error of at most 0.0003.
Values sent between devices are 32-bit elements; how exact they have to be, the bound alone decides.
A program may use at most 64 MiB of HBM per device.

```python
import math
import jax
import jax.numpy as jnp
from jax import lax

SPECIES = 17
REACT = 73
FIELDS = 18
CX = 4
GRID_CELLS_X = 512
GRID_CELLS_Y = 256
GRID_CELLS_Z = 16
N_GX = 128


def touch_ends(entries, stream_key, least, high):
    shape = entries.shape
    place = [jax.random.randint(jax.random.fold_in(stream_key, axis), (), 0, shape[axis]) for axis in range(len(shape))]
    entries = entries.at[tuple(place)].set(least)
    longest = shape.index(max(shape))
    place[longest] = (place[longest] + 1) % shape[longest]
    return entries.at[tuple(place)].set(high)


def steps_of(own_key, shape, pieces, least, largest):
    loudness, own = 1.0, jax.random.fold_in(own_key, 6)
    for axis_at, parts in pieces:
        draws = jnp.exp(jax.random.uniform(jax.random.fold_in(own, axis_at), (parts,), jnp.float32, least / len(pieces), largest / len(pieces)))
        loudness = loudness * jnp.repeat(draws, shape[axis_at] // parts).reshape([-1 if axis == axis_at else 1 for axis in range(len(shape))])
    return loudness


def setup_inputs(seed: int = 0) -> dict:
    splits = jax.random.split(jax.random.key(seed), 9)
    concentration_levels = jnp.clip(jnp.exp(math.log(1.0) - 9.2103404 * jax.random.uniform(splits[0], (3, SPECIES, GRID_CELLS_X, GRID_CELLS_Z, GRID_CELLS_Y), jnp.float32) ** steps_of(splits[0], (3, SPECIES, GRID_CELLS_X, GRID_CELLS_Z, GRID_CELLS_Y), ((2, 128), (3, 2), (4, 2)), -0.2, 0.2)), 0.0001, 1.0)
    thermal_levels = jnp.clip(4.0 + 2.0 * jax.random.uniform(splits[1], (3, GRID_CELLS_X, GRID_CELLS_Z, GRID_CELLS_Y), jnp.float32) ** steps_of(splits[1], (3, GRID_CELLS_X, GRID_CELLS_Z, GRID_CELLS_Y), ((1, 128), (2, 2), (3, 2)), -0.2, 0.2), 4.0, 6.0)
    fluid_velocity = jnp.clip(jax.random.uniform(splits[2], (3, GRID_CELLS_X, GRID_CELLS_Z, GRID_CELLS_Y), jnp.float32, -4.0, 4.0) * steps_of(splits[2], (3, GRID_CELLS_X, GRID_CELLS_Z, GRID_CELLS_Y), ((1, 128), (2, 2), (3, 2)), -0.4, 0.0), -4.0, 4.0)
    diffusivity = jnp.clip(jnp.exp(jax.random.uniform(splits[3], (FIELDS,), jnp.float32, math.log(0.15), math.log(0.6))), 0.15, 0.6)
    natural_logged_prefactors = jnp.clip(jax.random.uniform(splits[4], (REACT,), jnp.float32, -3.0, 0.0), -3.0, 0.0)
    energy_barrier_kelvin = jnp.clip(jnp.exp(jax.random.uniform(splits[5], (REACT,), jnp.float32, math.log(1.0), math.log(8.0))), 1.0, 8.0)
    enthalpy_yield_per_mole = jnp.clip(jax.random.uniform(splits[6], (SPECIES,), jnp.float32, -0.3, 0.3), -0.3, 0.3)
    stoichiometric_member_table = touch_ends(jax.random.randint(splits[7], (4, REACT), 0, SPECIES + 1), jax.random.fold_in(splits[7], 1), 0, SPECIES).astype(jnp.int32)
    return dict(concentration_levels=concentration_levels, thermal_levels=thermal_levels, fluid_velocity=fluid_velocity, diffusivity=diffusivity, natural_logged_prefactors=natural_logged_prefactors, energy_barrier_kelvin=energy_barrier_kelvin, enthalpy_yield_per_mole=enthalpy_yield_per_mole, stoichiometric_member_table=stoichiometric_member_table)


time_step = 0.125
first_coeffs = (4.0 / 5.0, -1.0 / 5.0, 4.0 / 105.0, -1.0 / 280.0)
second_coeffs = (8.0 / 5.0, -1.0 / 5.0, 8.0 / 315.0, -1.0 / 560.0)
center_coeff = -205.0 / 72.0


def stencils(padded, direction, length_cells):
    def shifted(offset):
        return lax.slice_in_dim(padded, 4 + offset, 4 + offset + length_cells, axis=direction)
    gradient = first_coeffs[0] * (shifted(1) - shifted(-1))
    curvature = center_coeff * shifted(0) + second_coeffs[0] * (shifted(1) + shifted(-1))
    for offset in range(1, 4):
        gradient = gradient + first_coeffs[offset] * (shifted(offset + 1) - shifted(-offset - 1))
        curvature = curvature + second_coeffs[offset] * (shifted(offset + 1) + shifted(-offset - 1))
    return gradient, curvature


def periodic(field, direction):
    extent = field.shape[direction]
    return jnp.concatenate([lax.slice_in_dim(field, extent - 4, extent, axis=direction), field,
                            lax.slice_in_dim(field, 0, 4, axis=direction)], axis=direction)


def combustion_source_terms(mixture_constituent, mixture_warmth_kelvin, natural_logged_prefactors, energy_barrier_kelvin, enthalpy_yield_per_mole, stoichiometric_member_table):
    count_species = mixture_constituent.shape[0]
    expanded_array_extent = (slice(None),) + (None,) * mixture_warmth_kelvin.ndim
    forward_speed_constants = jnp.exp(natural_logged_prefactors[expanded_array_extent] - energy_barrier_kelvin[expanded_array_extent] / mixture_warmth_kelvin[None])
    partner = jnp.mean(mixture_constituent, axis=0)
    lookup = jnp.concatenate([mixture_constituent, partner[None]], axis=0)
    progress = forward_speed_constants * jnp.take(lookup, stoichiometric_member_table[0], axis=0) * jnp.take(lookup, stoichiometric_member_table[1], axis=0)
    labels = jnp.arange(count_species + 1, dtype=jnp.int32)[:, None]

    def onehot(which_row):
        return (labels == stoichiometric_member_table[which_row][None, :]).astype(jnp.float32)

    stoich = (onehot(2) + onehot(3) - onehot(0) - onehot(1))[:count_species]
    production = jnp.tensordot(stoich, progress, axes=1, precision=lax.Precision.HIGHEST)
    release = jnp.tensordot(enthalpy_yield_per_mole, production, axes=1, precision=lax.Precision.HIGHEST)
    return production, release


def tendency(extended, padded_z, padded_y, interior, velocity, diffusivity, natural_logged_prefactors, energy_barrier_kelvin, enthalpy_yield_per_mole, stoichiometric_member_table):
    count_species = interior.shape[0] - 1
    grad_x, curv_x = stencils(extended, 1, interior.shape[1])
    grad_z, curv_z = stencils(padded_z, 2, interior.shape[2])
    grad_y, curv_y = stencils(padded_y, 3, interior.shape[3])
    transport = velocity[0][None] * grad_x + velocity[1][None] * grad_y + velocity[2][None] * grad_z
    laplace = curv_x + curv_y + curv_z
    diffusion = diffusivity[:, None, None, None]
    change = diffusion * laplace - transport
    production, release = combustion_source_terms(interior[:count_species], interior[count_species], natural_logged_prefactors,
                                    energy_barrier_kelvin, enthalpy_yield_per_mole, stoichiometric_member_table)
    return jnp.concatenate([change[:count_species] + production,
                            (change[count_species] + release)[None]], axis=0)


def full_tendency(state, delayed_state, velocity, constants):
    pad_state = periodic(state, 1)
    pad_late = periodic(delayed_state, 1)

    def one_block(block_index):
        offset = block_index * CX
        current = lax.dynamic_slice_in_dim(pad_state, offset, CX + 8, axis=1)
        delayed = lax.dynamic_slice_in_dim(pad_late, offset, CX + 8, axis=1)
        interior = current[:, 4:4 + CX]
        extended = jnp.concatenate([delayed[:, :4], interior, delayed[:, 4 + CX:]], axis=1)
        velocity_block = lax.dynamic_slice_in_dim(velocity, offset, CX, axis=1)
        return tendency(extended, periodic(interior, 2), periodic(interior, 3), interior, velocity_block, *constants)

    blocks = lax.map(one_block, jnp.arange(N_GX, dtype=jnp.int32))
    moved = jnp.moveaxis(blocks, 0, 1)
    return moved.reshape((state.shape[0], state.shape[1], state.shape[2], state.shape[3]))


def advance(current, newer, older, velocity, constants):
    first_rate = full_tendency(current, 2.0 * newer - older, velocity, constants)
    predictor = current + time_step * first_rate
    second_rate = full_tendency(predictor, 3.0 * newer - 2.0 * older, velocity, constants)
    return current + (0.5 * time_step) * (first_rate + second_rate)


def reference(concentration_levels, thermal_levels, fluid_velocity, diffusivity, natural_logged_prefactors, energy_barrier_kelvin, enthalpy_yield_per_mole, stoichiometric_member_table):
    count_species = concentration_levels.shape[1]
    time_levels = [jnp.concatenate([concentration_levels[level_index], thermal_levels[level_index][None]], axis=0)
              for level_index in range(3)]
    constants = (diffusivity, natural_logged_prefactors, energy_barrier_kelvin, enthalpy_yield_per_mole, stoichiometric_member_table)
    stepped = advance(time_levels[2], time_levels[1], time_levels[0], fluid_velocity, constants)
    final_state = advance(stepped, time_levels[2], time_levels[1], fluid_velocity, constants)
    return final_state[:count_species], final_state[count_species]
```

```python
import functools

import jax
import jax.numpy as jnp
import numpy as np
from jax import lax
from jax.experimental import pallas as pl
from jax.experimental.pallas import tpu as pltpu
from jax.sharding import PartitionSpec as P

SPECIES = 17
FIELDS = 18
REACT = 73
CX = 4
CZ = 8
CY = 128
ROWS = FIELDS * CZ
LANES = CX * CY
QUAD = 4
QUADS = (FIELDS + QUAD - 1) // QUAD
QROWS = 640
CHUNKS = ((0, 8), (8, 16), (16, 18))

time_step = 0.125
first_coeffs = (4.0 / 5.0, -1.0 / 5.0, 4.0 / 105.0, -1.0 / 280.0)
second_coeffs = (8.0 / 5.0, -1.0 / 5.0, 8.0 / 315.0, -1.0 / 560.0)
center_coeff = -205.0 / 72.0

MESH = pl.DeviceIdType.MESH


FIRST_SCALE = 840.0
SECOND_SCALE = 5040.0
first_scaled = (672.0, -168.0, 32.0, -3.0)
second_scaled = (8064.0, -1008.0, 128.0, -9.0)


def weight(distance):
    size = abs(distance)
    if size == 0 or size > 4:
        return 0.0, 0.0
    sign = 1.0 if distance > 0 else -1.0
    return sign * first_coeffs[size - 1], second_coeffs[size - 1]


def scaled(distance):
    size = abs(distance)
    if size == 0 or size > 4:
        return 0.0, 0.0
    sign = 1.0 if distance > 0 else -1.0
    return sign * first_scaled[size - 1], second_scaled[size - 1]


def y_matrix():
    matrix = np.zeros((CY, 2 * CY), np.float32)
    for out in range(CY):
        for at in range(CY):
            matrix[at, out], matrix[at, CY + out] = scaled(at - out)
    return np.concatenate([matrix, matrix])


def edge_matrix():
    matrix = np.zeros((CY, 2 * CY), np.float32)
    for base in range(0, CY, 8):
        for at in range(8):
            for out in range(8):
                if (at < 4) != (out < 4):
                    first, second = scaled(at - out)
                    matrix[base + at, base + out] = first
                    matrix[base + at, CY + base + out] = second
    return np.concatenate([matrix, matrix])


def z_matrix():
    half = QUAD * CZ
    matrix = np.zeros((2 * half, 2 * half), np.float32)
    for slab in range(QUAD):
        for out in range(CZ):
            for step in range(-4, 5):
                at = out + step
                column = slab * CZ + at % CZ + (0 if 0 <= at < CZ else half)
                first, second = scaled(step)
                matrix[slab * CZ + out, column] += first
                matrix[half + slab * CZ + out, column] += second
    return np.concatenate([matrix, matrix], axis=1)


def split(value):
    high = value.astype(jnp.bfloat16)
    return high, (value - high.astype(jnp.float32)).astype(jnp.bfloat16)


def dot(left, right):
    return jnp.dot(left, right, preferred_element_type=jnp.float32)


def kernel(
    n_gx,
    conc, therm, veloc, table_h, logs_h, barriers_h, heats_h, kappas_h, ymat_h, emat_h, zmat_h,
    conc_out, therm_out,
    past, lev_a, lev_n, lev_c, vel, xhalo, xterm, state1, state2, state3, zhalo, ypack, yhalo,
    rate, local, result, qbuf, made, parts, near, dy, dz1, dz2, edge, kpack, vpack, nuk,
    ymat, emat, zmat, ymat_v, emat_v, zmat_v,
    table_s, logs, barriers, heats, kappas, table_v,
    past_sem, ld_sem, vel_send, swap_send, arrive, x_send, x_recv, z_send, z_recv, y_send, y_recv,
    o_send, o_recv,
):
    gx, gy, gz = lax.axis_index("gx"), lax.axis_index("gy"), lax.axis_index("gz")
    period = max(n_gx // 8, 1)

    def half_of(at):
        return lax.rem(lax.div(at, period), 2)

    mirrored = half_of(gx)
    moves = lax.rem(gy + gz + mirrored, 2) == 1

    def x_beside(at):
        flips = half_of(at) != mirrored
        return {
            "gx": at,
            "gy": jnp.where(flips, 1 - gy, gy),
            "gz": jnp.where(flips, 1 - gz, gz),
        }

    right = x_beside(lax.rem(gx + 1, n_gx))
    left = x_beside(lax.rem(gx + n_gx - 1, n_gx))
    z_partner = {"gx": gx, "gy": 1 - gy, "gz": gz}
    y_partner = {"gx": gx, "gy": gy, "gz": 1 - gz}
    opposite = {"gx": gx, "gy": 1 - gy, "gz": 1 - gz}

    def remote(src, dst, send, recv, where):
        return pltpu.make_async_remote_copy(
            src_ref=src, dst_ref=dst, send_sem=send, recv_sem=recv,
            device_id=where, device_id_type=MESH,
        )

    past_loads = []
    for chunk, (begin, end) in enumerate(CHUNKS):
        stop = min(end, SPECIES)
        copies = [(conc.at[0:2, begin:stop], past.at[:, begin:stop])]
        if end == FIELDS:
            copies.append((therm.at[0:2], past.at[:, SPECIES]))
        past_loads.append([
            pltpu.make_async_copy(src, dst, past_sem.at[chunk, at])
            for at, (src, dst) in enumerate(copies)
        ])
    shared = ((table_h, table_v), (ymat_h, ymat_v), (emat_h, emat_v), (zmat_h, zmat_v), (table_h, table_s),
              (logs_h, logs), (barriers_h, barriers), (heats_h, heats), (kappas_h, kappas))
    loads = [
        pltpu.make_async_copy(src, dst, ld_sem.at[at]) for at, (src, dst) in enumerate(shared)
    ]
    for copy in [copy for copies in past_loads for copy in copies] + loads:
        copy.start()

    barrier = pltpu.get_barrier_semaphore()
    for where in (left, right, z_partner, y_partner, opposite):
        pl.semaphore_signal(barrier, inc=1, device_id=where, device_id_type=MESH)

    def moved(level, chunk):
        begin, end = CHUNKS[chunk]
        if level == 0:
            return [(past.at[0, begin:end], lev_a.at[begin:end])]
        into = (lev_n, lev_c)[level - 1]
        stop = min(end, SPECIES)
        copies = [(conc.at[level, begin:stop], into.at[begin:stop])]
        if end == FIELDS:
            copies.append((therm.at[level], into.at[SPECIES]))
        return copies

    def swaps(level, chunk):
        return [
            remote(src, dst, swap_send.at[level, chunk, at], arrive.at[level, chunk, at], opposite)
            for at, (src, dst) in enumerate(moved(level, chunk))
        ]

    def own(level, chunk):
        return [
            pltpu.make_async_copy(src, dst, arrive.at[level, chunk, at])
            for at, (src, dst) in enumerate(moved(level, chunk))
        ]

    def placed(level, chunk):
        for at, (src, dst) in enumerate(moved(level, chunk)):
            pltpu.make_async_copy(dst, dst, arrive.at[level, chunk, at]).wait()

    vel_swap = remote(veloc, vel, vel_send.at[0], vel_send.at[1], opposite)
    vel_own = pltpu.make_async_copy(veloc, vel, vel_send.at[1])

    levels = (lev_a, lev_n, lev_c)

    def x_copies(level, chunk, source=None):
        begin, end = CHUNKS[chunk]
        src = (levels[level] if source is None else source).at[begin:end]
        return [
            remote(
                src, xhalo.at[level, side, begin:end],
                x_send.at[level, side, chunk], x_recv.at[level, side, chunk], where,
            )
            for side, where in ((0, right), (1, left))
        ]

    def delay(chunk):
        for copy in past_loads[chunk]:
            copy.wait()

        def one(field, carry):
            past[0, field] = 2.0 * past[1, field] - past[0, field]
            return carry

        lax.fori_loop(*CHUNKS[chunk], one, 0, unroll=2)

    def start(copies):
        for copy in copies:
            copy.start()

    stays = jnp.logical_not(moves)
    chunks = range(len(CHUNKS))

    pl.semaphore_wait(barrier, 5)

    @pl.when(stays)
    def _():
        vel_own.start()
        for chunk in chunks:
            start(own(2, chunk))
        for chunk in chunks:
            delay(chunk)
            start(x_copies(0, chunk, past.at[0]))
        for chunk in chunks:
            start(x_copies(1, chunk, past.at[1]))

    @pl.when(moves)
    def _():
        vel_swap.start()
        for chunk in chunks:
            delay(chunk)
            start(swaps(0, chunk))
        for chunk in chunks:
            start(swaps(2, chunk))
        for chunk in chunks:
            start(swaps(1, chunk))

    for load in loads:
        load.wait()
    for matrix, into in ((ymat_v, ymat), (emat_v, emat), (zmat_v, zmat)):
        into[...] = matrix[...].astype(jnp.bfloat16)

    filler = jnp.full((4, CY - REACT), 31.0, jnp.float32)
    members = jnp.concatenate([table_v[...].astype(jnp.float32), filler], axis=1)
    members = jnp.concatenate([members, jnp.zeros((12, CY), jnp.float32)], axis=0)
    column = lax.broadcasted_iota(jnp.int32, (CY, 2 * QROWS), 1)
    column = jnp.where(column >= QROWS, column - QROWS, column)
    reaction = lax.broadcasted_iota(jnp.int32, (CY, 2 * QROWS), 0)
    spread = jnp.where(lax.shift_right_logical(column, 3) == reaction, 1.0, 0.0)
    members = dot(members.astype(jnp.bfloat16), spread.astype(jnp.bfloat16))
    level_z = lax.broadcasted_iota(jnp.int32, (CZ, 2 * QROWS), 0)
    same_z = (lax.broadcasted_iota(jnp.int32, (CZ, 2 * QROWS), 1) & 7) == level_z
    for species in range(0, FIELDS, 2):
        both = []
        for at in (species, species + 1):
            total = jnp.zeros((1, 2 * QROWS), jnp.float32)
            if at < SPECIES:
                for which, sign in ((0, -1.0), (1, -1.0), (2, 1.0), (3, 1.0)):
                    total = total + jnp.where(members[which : which + 1] == at, sign, 0.0)
            both.append(jnp.where(same_z, total, 0.0))
        rows = slice(CZ * species, CZ * species + 2 * CZ)
        nuk[rows, :] = jnp.concatenate(both, axis=0).astype(jnp.bfloat16)
    filled = (REACT + 1) * CZ
    for begin in (filled, QROWS + filled):
        qbuf[begin : begin + QROWS - filled, :] = jnp.zeros((QROWS - filled, LANES), jnp.bfloat16)

    lane_block = lax.broadcasted_iota(jnp.int32, (CZ, CY), 1) // 8
    lane = lax.broadcasted_iota(jnp.int32, (CZ, CY), 1)
    at_edge = jnp.logical_or(lane < 4, lane >= CY - 4)
    for quad in range(QUADS):
        packed = jnp.zeros((CZ, CY), jnp.float32)
        for slab in range(min(QUAD, FIELDS - QUAD * quad)):
            packed = jnp.where(
                lane_block // CX == slab, kappas[0, QUAD * quad + slab], packed
            )
        kpack[quad] = packed * (1.0 / SECOND_SCALE)

    @pl.when(moves)
    def _():
        for chunk in chunks:
            placed(0, chunk)
            start(x_copies(0, chunk))

    def z_copy(k, state, chunk):
        begin, end = CHUNKS[chunk]
        return remote(
            state.at[begin:end], zhalo.at[k, begin:end], z_send.at[k, chunk], z_recv.at[k, chunk],
            z_partner,
        )

    def y_copy(k):
        return remote(ypack.at[k], yhalo.at[k], y_send.at[k], y_recv.at[k], y_partner)

    def pack(columns):
        packed = jnp.zeros((CZ, CY), jnp.float32)
        for at, value in enumerate(columns):
            packed = jnp.where(lane_block == at, pltpu.roll(value, (8 * at + 4) % CY, 1), packed)
        return packed

    def send_borders(k, state, chunk):
        z_copy(k, state, chunk).start()
        begin, end = CHUNKS[chunk]
        for first in range(begin, end, QUAD):
            fields = range(first, min(first + QUAD, end))
            ypack[k, first // QUAD] = pack([state[f, x] for f in fields for x in range(CX)])
        if end == FIELDS:
            y_copy(k).start()

    def reactions(state):
        total = state[0]
        for species in range(1, SPECIES):
            total = total + state[species]
        state[FIELDS] = total * (1.0 / SPECIES)
        inverse = 1.0 / state[SPECIES]

        def two(pair, carry):
            both = []
            for at in range(2):
                j = jnp.minimum(2 * pair + at, REACT - 1)
                first, second = table_s[0, j], table_s[1, j]
                first = jnp.where(first == SPECIES, FIELDS, first)
                second = jnp.where(second == SPECIES, FIELDS, second)
                speed = jnp.exp(logs[0, j] - barriers[0, j] * inverse)
                both.append(speed * state[first] * state[second])
            begin = pl.multiple_of(16 * pair, 16)
            for x in range(CX):
                high, low = split(jnp.concatenate([both[0][x], both[1][x]], axis=0))
                lanes = slice(CY * x, CY * x + CY)
                qbuf[pl.ds(begin, 16), lanes] = high
                qbuf[pl.ds(QROWS + begin, 16), lanes] = low
            return carry

        lax.fori_loop(0, (REACT + 1) // 2, two, 0, unroll=2)

    def in_parts(source, into):
        for f in range(0, FIELDS, 2):
            for x in range(CX):
                value = jnp.concatenate([source[f, x], source[f + 1, x]], axis=0)
                into[x, CZ * f : CZ * f + 16, 0:CY], into[x, CZ * f : CZ * f + 16, CY:] = split(
                    value
                )

    def transport(k, state, finish, done=None):
        in_parts(state, parts)
        made[...] = dot(nuk[...], qbuf[...]).reshape(FIELDS, CZ, LANES)
        for x in range(CX):
            dy[x] = dot(parts[x], ymat[...]).reshape(FIELDS, CZ, 2 * CY)
        for chunk in chunks:
            z_copy(k, state, chunk).wait_recv()
        in_parts(zhalo.at[k], near)
        for first in (0, 4, 8, 12, 14):
            rows = slice(CZ * first, CZ * (first + QUAD))
            for x in range(0, CX, 2):
                sides = []
                for at in (x, x + 1):
                    sides.append(jnp.concatenate(
                        [parts[at, rows, 0:CY], near[at, rows, 0:CY],
                         parts[at, rows, CY:], near[at, rows, CY:]], axis=0,
                    ))
                out = dot(zmat[...], jnp.concatenate(sides, axis=1))
                lanes = slice(CY * x, CY * x + 2 * CY)
                dz1[first : first + QUAD, :, lanes] = out[: QUAD * CZ].reshape(QUAD, CZ, 2 * CY)
                dz2[first : first + QUAD, :, lanes] = out[QUAD * CZ :].reshape(QUAD, CZ, 2 * CY)
        y_copy(k).wait_recv()
        value = jnp.concatenate(
            [yhalo[k].reshape(QUADS * CZ, CY), jnp.zeros((CZ, CY), jnp.float32)], axis=0
        )
        out = dot(jnp.concatenate(split(value), axis=1), emat[...])
        for quad in range(QUADS):
            part = out[CZ * quad : CZ * quad + CZ]
            edge[quad] = kpack[quad] * part[:, CY:] - vpack[...] * part[:, 0:CY]

        def one(f, x, packed, at, source):
            values = [state[f, q] for q in range(CX)]
            grad, curv = None, (3.0 * center_coeff) * values[x]
            for q in range(CX):
                if q != x:
                    first, second = weight(q - x)
                    curv = curv + second * values[q]
                    grad = first * values[q] if grad is None else grad + first * values[q]
            lanes = slice(CY * x, CY * x + CY)
            curv = curv + (1.0 / SECOND_SCALE) * (dy[x, f, :, CY:] + dz2[f, :, lanes])
            along = vel[0, x] * grad + vel[1, x] * dy[x, f, :, 0:CY] + vel[2, x] * dz1[f, :, lanes]
            border = pltpu.roll(packed, (CY - (8 * at + 4)) % CY, 1)
            source = source + jnp.where(at_edge, border, 0.0)
            finish(f, x, kappas[0, f] * curv - along + source)

        def quad_of_fields(quad, release, fields=QUAD):
            release = list(release)
            packed = edge[quad]
            for slab in range(fields):
                f = QUAD * quad + slab
                for x in range(CX):
                    at = slab * CX + x
                    if slab == 1 and fields == 2:
                        one(f, x, packed, at, release[x])
                        continue
                    source = made[f, :, CY * x : CY * x + CY]
                    release[x] = release[x] + heats[0, f] * source
                    one(f, x, packed, at, source)
            return tuple(release)

        release = (jnp.zeros((CZ, CY), jnp.float32),) * CX
        for chunk, (begin, end) in enumerate(CHUNKS):
            release = lax.fori_loop(begin // QUAD, end // QUAD, quad_of_fields, release)
            if end == FIELDS:
                quad_of_fields(QUADS - 1, release, fields=2)
            if done is not None:
                done(chunk)

    def x_halo(level, make, done):
        def one(f, carry):
            before = [xhalo[level, 0, f, q] for q in range(CX)]
            after = [xhalo[level, 1, f, q] for q in range(CX)]
            for x in range(CX):
                grad = curv = None
                for q in range(CX):
                    for value, distance in ((before[q], q - 4 - x), (after[q], q + 4 - x)):
                        first, second = weight(distance)
                        if second == 0.0:
                            continue
                        grad = first * value if grad is None else grad + first * value
                        curv = second * value if curv is None else curv + second * value
                make(f, x, kappas[0, f] * curv - vel[0, x] * grad)
            return carry

        for chunk in chunks:
            for copy in x_copies(level, chunk):
                copy.wait_recv()
            lax.fori_loop(*CHUNKS[chunk], one, 0, unroll=2)
            done(chunk)

    def keep(f, x, value):
        local[f, x] = value

    for chunk in chunks:
        placed(2, chunk)
        send_borders(0, lev_c, chunk)
    reactions(lev_c)

    @pl.when(stays)
    def _():
        for chunk in chunks:
            start(x_copies(2, chunk))

    @pl.when(moves)
    def _():
        for chunk in chunks:
            placed(1, chunk)
            start(x_copies(1, chunk))

    vel_own.wait()
    for x in range(CX):
        vel[1, x] = vel[1, x] * (1.0 / FIRST_SCALE)
        vel[2, x] = vel[2, x] * (1.0 / FIRST_SCALE)
    vpack[...] = pack([vel[1, x] for x in range(CX)] * QUAD)
    transport(0, lev_c, keep)

    @pl.when(moves)
    def _():
        for chunk in chunks:
            start(x_copies(2, chunk))

    def make(f, x, share):
        xterm[0, f, x] = share
        value = local[f, x] + share
        rate[f, x] = value
        state1[f, x] = lev_c[f, x] + time_step * value

    x_halo(0, make, lambda chunk: send_borders(1, state1, chunk))

    reactions(state1)
    transport(1, state1, keep)

    def make(f, x, share):
        xterm[1, f, x] = share
        value = local[f, x] + 2.0 * xterm[0, f, x] - share
        state2[f, x] = lev_c[f, x] + 0.5 * time_step * (rate[f, x] + value)

    x_halo(1, make, lambda chunk: send_borders(2, state2, chunk))

    reactions(state2)
    transport(2, state2, keep)

    def make(f, x, late):
        before = xterm[1, f, x]
        value = local[f, x] + 2.0 * late - before
        state3[f, x] = state2[f, x] + time_step * value
        rate[f, x] = value + 3.0 * late - 2.0 * before

    x_halo(2, make, lambda chunk: send_borders(3, state3, chunk))

    reactions(state3)

    def last(f, x, value):
        result[f, x] = state2[f, x] + 0.5 * time_step * (rate[f, x] + value)

    def outs(chunk):
        begin, end = CHUNKS[chunk]
        stop = min(end, SPECIES)
        copies = [(result.at[begin:stop], conc_out.at[begin:stop])]
        if end == FIELDS:
            copies.append((result.at[SPECIES], therm_out))
        return copies

    def out_swaps(chunk):
        return [
            remote(src, dst, o_send.at[chunk, at], o_recv.at[chunk, at], opposite)
            for at, (src, dst) in enumerate(outs(chunk))
        ]

    def out_own(chunk):
        return [
            pltpu.make_async_copy(src, dst, o_recv.at[chunk, at])
            for at, (src, dst) in enumerate(outs(chunk))
        ]

    def done(chunk):
        @pl.when(moves)
        def _():
            start(out_swaps(chunk))

        @pl.when(stays)
        def _():
            start(out_own(chunk))

    transport(3, state3, last, done)

    for level in range(3):
        for chunk in chunks:
            for copy in x_copies(level, chunk):
                copy.wait_send()
    for k, state in enumerate((lev_c, state1, state2, state3)):
        for chunk in chunks:
            z_copy(k, state, chunk).wait_send()
        y_copy(k).wait_send()

    @pl.when(moves)
    def _():
        vel_swap.wait_send()
        for chunk in chunks:
            for copy in swaps(0, chunk) + swaps(1, chunk) + swaps(2, chunk) + out_swaps(chunk):
                copy.wait_send()

    for chunk in chunks:
        for at, (src, dst) in enumerate(outs(chunk)):
            pltpu.make_async_copy(dst, dst, o_recv.at[chunk, at]).wait()


def local(
    concentration_levels,
    thermal_levels,
    fluid_velocity,
    diffusivity,
    natural_logged_prefactors,
    energy_barrier_kelvin,
    enthalpy_yield_per_mole,
    stoichiometric_member_table,
):
    n_gx = lax.axis_size("gx")
    any_space = pl.BlockSpec(memory_space=pl.ANY)
    f32, bf16 = jnp.float32, jnp.bfloat16
    block = (FIELDS, CX, CZ, CY)
    wide = (FIELDS + 1, CX, CZ, CY)
    parts = len(CHUNKS)
    dma = pltpu.SemaphoreType.DMA
    scratch = [
        pltpu.VMEM((2,) + block, f32),
        pltpu.VMEM(block, f32),
        pltpu.VMEM(block, f32),
        pltpu.VMEM(wide, f32),
        pltpu.VMEM((3, CX, CZ, CY), f32),
        pltpu.VMEM((3, 2) + block, f32),
        pltpu.VMEM((2,) + block, f32),
        pltpu.VMEM(wide, f32),
        pltpu.VMEM(wide, f32),
        pltpu.VMEM(wide, f32),
        pltpu.VMEM((4,) + block, f32),
        pltpu.VMEM((4, QUADS, CZ, CY), f32),
        pltpu.VMEM((4, QUADS, CZ, CY), f32),
        pltpu.VMEM(block, f32),
        pltpu.VMEM(block, f32),
        pltpu.VMEM(block, f32),
        pltpu.VMEM((2 * QROWS, LANES), bf16),
        pltpu.VMEM((FIELDS, CZ, LANES), f32),
        pltpu.VMEM((CX, ROWS, 2 * CY), bf16),
        pltpu.VMEM((CX, ROWS, 2 * CY), bf16),
        pltpu.VMEM((CX, FIELDS, CZ, 2 * CY), f32),
        pltpu.VMEM((FIELDS, CZ, LANES), f32),
        pltpu.VMEM((FIELDS, CZ, LANES), f32),
        pltpu.VMEM((QUADS, CZ, CY), f32),
        pltpu.VMEM((QUADS, CZ, CY), f32),
        pltpu.VMEM((CZ, CY), f32),
        pltpu.VMEM((ROWS, 2 * QROWS), bf16),
        pltpu.VMEM((2 * CY, 2 * CY), bf16),
        pltpu.VMEM((2 * CY, 2 * CY), bf16),
        pltpu.VMEM((2 * QUAD * CZ, 4 * QUAD * CZ), bf16),
        pltpu.VMEM((2 * CY, 2 * CY), f32),
        pltpu.VMEM((2 * CY, 2 * CY), f32),
        pltpu.VMEM((2 * QUAD * CZ, 4 * QUAD * CZ), f32),
        pltpu.SMEM((4, REACT), jnp.int32),
        pltpu.SMEM((1, REACT), f32),
        pltpu.SMEM((1, REACT), f32),
        pltpu.SMEM((1, SPECIES), f32),
        pltpu.SMEM((1, FIELDS), f32),
        pltpu.VMEM((4, REACT), jnp.int32),
        dma((parts, 2)),
        dma((9,)),
        dma((2,)),
        dma((3, parts, 2)),
        dma((3, parts, 2)),
        dma((3, 2, parts)),
        dma((3, 2, parts)),
        dma((4, parts)),
        dma((4, parts)),
        dma((4,)),
        dma((4,)),
        dma((parts, 2)),
        dma((parts, 2)),
    ]
    return pl.pallas_call(
        functools.partial(kernel, n_gx),
        out_shape=(
            jax.ShapeDtypeStruct((SPECIES, CX, CZ, CY), f32),
            jax.ShapeDtypeStruct((CX, CZ, CY), f32),
        ),
        in_specs=[any_space] * 11,
        out_specs=(any_space, any_space),
        scratch_shapes=scratch,
        compiler_params=pltpu.CompilerParams(
            collective_id=0, has_side_effects=True, vmem_limit_bytes=64 * 1024 * 1024
        ),
    )(
        concentration_levels,
        thermal_levels,
        fluid_velocity,
        stoichiometric_member_table,
        natural_logged_prefactors[None],
        energy_barrier_kelvin[None],
        enthalpy_yield_per_mole[None],
        diffusivity[None],
        jnp.asarray(y_matrix()),
        jnp.asarray(edge_matrix()),
        jnp.asarray(z_matrix()),
    )


def solution(mesh):
    in_specs = (
        P(None, None, "gx", "gz", "gy"),
        P(None, "gx", "gz", "gy"),
        P(None, "gx", "gz", "gy"),
        P(),
        P(),
        P(),
        P(),
        P(),
    )
    out_specs = (P(None, "gx", "gz", "gy"), P("gx", "gz", "gy"))
    return jax.shard_map(local, mesh=mesh, in_specs=in_specs, out_specs=out_specs, check_vma=False)
```

```python
import functools

import jax
import jax.numpy as jnp
import numpy as np
from jax import lax
from jax.experimental import pallas as pl
from jax.experimental.pallas import tpu as pltpu
from jax.sharding import PartitionSpec as P

SPECIES = 17
FIELDS = 18
REACT = 73
CX = 4
CZ = 8
CY = 128
ROWS = FIELDS * CZ
LANES = CX * CY
QUAD = 4
QUADS = (FIELDS + QUAD - 1) // QUAD
QROWS = 640
CHUNKS = ((0, 8), (8, 16), (16, 18))

time_step = 0.125
first_coeffs = (4.0 / 5.0, -1.0 / 5.0, 4.0 / 105.0, -1.0 / 280.0)
second_coeffs = (8.0 / 5.0, -1.0 / 5.0, 8.0 / 315.0, -1.0 / 560.0)
center_coeff = -205.0 / 72.0

MESH = pl.DeviceIdType.MESH


FIRST_SCALE = 840.0
SECOND_SCALE = 5040.0
first_scaled = (672.0, -168.0, 32.0, -3.0)
second_scaled = (8064.0, -1008.0, 128.0, -9.0)


def weight(distance):
    size = abs(distance)
    if size == 0 or size > 4:
        return 0.0, 0.0
    sign = 1.0 if distance > 0 else -1.0
    return sign * first_coeffs[size - 1], second_coeffs[size - 1]


def scaled(distance):
    size = abs(distance)
    if size == 0 or size > 4:
        return 0.0, 0.0
    sign = 1.0 if distance > 0 else -1.0
    return sign * first_scaled[size - 1], second_scaled[size - 1]


def y_matrix():
    matrix = np.zeros((CY, 2 * CY), np.float32)
    for out in range(CY):
        for at in range(CY):
            matrix[at, out], matrix[at, CY + out] = scaled(at - out)
    return np.concatenate([matrix, matrix])


def edge_matrix():
    matrix = np.zeros((CY, 2 * CY), np.float32)
    for base in range(0, CY, 8):
        for at in range(8):
            for out in range(8):
                if (at < 4) != (out < 4):
                    first, second = scaled(at - out)
                    matrix[base + at, base + out] = first
                    matrix[base + at, CY + base + out] = second
    return np.concatenate([matrix, matrix])


def z_matrix():
    half = QUAD * CZ
    matrix = np.zeros((2 * half, 2 * half), np.float32)
    for slab in range(QUAD):
        for out in range(CZ):
            for step in range(-4, 5):
                at = out + step
                column = slab * CZ + at % CZ + (0 if 0 <= at < CZ else half)
                first, second = scaled(step)
                matrix[slab * CZ + out, column] += first
                matrix[half + slab * CZ + out, column] += second
    return np.concatenate([matrix, matrix], axis=1)


def split(value):
    high = value.astype(jnp.bfloat16)
    return high, (value - high.astype(jnp.float32)).astype(jnp.bfloat16)


def dot(left, right):
    return jnp.dot(left, right, preferred_element_type=jnp.float32)


def kernel(
    n_gx,
    conc, therm, veloc, table_h, logs_h, barriers_h, heats_h, kappas_h, ymat_h, emat_h, zmat_h,
    next_out,
    past, lev_a, lev_n, lev_c, vel, xhalo, xterm, state1, state2, state3, zhalo, ypack, yhalo,
    rate, local, result, qbuf, made, parts, near, dy, dz1, dz2, edge, kpack, vpack, nuk,
    ymat, emat, zmat, ymat_v, emat_v, zmat_v,
    table_s, logs, barriers, heats, kappas, table_v,
    vel_near, past_sem, ld_sem, vel_send, swap_send, arrive, x_send, x_recv, z_send, z_recv, y_send, y_recv,
    o_send, o_recv,
):
    gx, gy, gz = lax.axis_index("gx"), lax.axis_index("gy"), lax.axis_index("gz")
    period = max(n_gx // 8, 1)

    def half_of(at):
        return lax.rem(lax.div(at, period), 2)

    mirrored = half_of(gx)
    moves = lax.rem(gy + gz + mirrored, 2) == 1

    def x_beside(at):
        flips = half_of(at) != mirrored
        return {
            "gx": at,
            "gy": jnp.where(flips, 1 - gy, gy),
            "gz": jnp.where(flips, 1 - gz, gz),
        }

    right = x_beside(lax.rem(gx + 1, n_gx))
    left = x_beside(lax.rem(gx + n_gx - 1, n_gx))
    z_partner = {"gx": gx, "gy": 1 - gy, "gz": gz}
    y_partner = {"gx": gx, "gy": gy, "gz": 1 - gz}
    opposite = {"gx": gx, "gy": 1 - gy, "gz": 1 - gz}

    def remote(src, dst, send, recv, where):
        return pltpu.make_async_remote_copy(
            src_ref=src, dst_ref=dst, send_sem=send, recv_sem=recv,
            device_id=where, device_id_type=MESH,
        )

    past_loads = []
    for chunk, (begin, end) in enumerate(CHUNKS):
        stop = min(end, SPECIES)
        copies = [(conc.at[:, begin:stop], past.at[:, begin:stop])]
        if end == FIELDS:
            copies.append((therm, past.at[:, SPECIES]))
        past_loads.append([
            pltpu.make_async_copy(src, dst, past_sem.at[chunk, at])
            for at, (src, dst) in enumerate(copies)
        ])
    shared = ((table_h, table_v), (ymat_h, ymat_v), (emat_h, emat_v), (zmat_h, zmat_v), (table_h, table_s),
              (logs_h, logs), (barriers_h, barriers), (heats_h, heats), (kappas_h, kappas),
              (veloc, vel_near))
    loads = [
        pltpu.make_async_copy(src, dst, ld_sem.at[at]) for at, (src, dst) in enumerate(shared)
    ]
    for copy in [copy for copies in past_loads for copy in copies] + loads:
        copy.start()

    barrier = pltpu.get_barrier_semaphore()
    for where in (left, right, z_partner, y_partner, opposite):
        pl.semaphore_signal(barrier, inc=1, device_id=where, device_id_type=MESH)

    def moved(level, chunk):
        begin, end = CHUNKS[chunk]
        return past.at[level, begin:end], (lev_a, lev_n, lev_c)[level].at[begin:end]

    def swap(level, chunk):
        src, dst = moved(level, chunk)
        return remote(src, dst, swap_send.at[level, chunk], arrive.at[level, chunk], opposite)

    def own(level, chunk):
        src, dst = moved(level, chunk)
        return pltpu.make_async_copy(src, dst, arrive.at[level, chunk])

    def placed(level, chunk):
        src, dst = moved(level, chunk)
        pltpu.make_async_copy(dst, dst, arrive.at[level, chunk]).wait()

    vel_swap = remote(vel_near, vel, vel_send.at[0], vel_send.at[1], opposite)
    vel_own = pltpu.make_async_copy(vel_near, vel, vel_send.at[1])

    levels = (lev_a, lev_n, lev_c)

    def x_copies(level, chunk, source=None):
        begin, end = CHUNKS[chunk]
        src = (levels[level] if source is None else source).at[begin:end]
        return [
            remote(
                src, xhalo.at[level, side, begin:end],
                x_send.at[level, side, chunk], x_recv.at[level, side, chunk], where,
            )
            for side, where in ((0, right), (1, left))
        ]

    def delay(chunk):
        for copy in past_loads[chunk]:
            copy.wait()

        def one(field, carry):
            past[0, field] = 2.0 * past[1, field] - past[0, field]
            return carry

        lax.fori_loop(*CHUNKS[chunk], one, 0, unroll=2)

    def start(copies):
        for copy in copies:
            copy.start()

    stays = jnp.logical_not(moves)
    chunks = range(len(CHUNKS))

    for chunk in chunks:
        delay(chunk)
    loads[-1].wait()
    pl.semaphore_wait(barrier, 5)

    @pl.when(stays)
    def _():
        vel_own.start()
        for chunk in chunks:
            own(2, chunk).start()
        for chunk in chunks:
            start(x_copies(0, chunk, past.at[0]))

    @pl.when(moves)
    def _():
        for chunk in chunks:
            swap(0, chunk).start()
        vel_swap.start()
        for level in (2, 1):
            for chunk in chunks:
                swap(level, chunk).start()

    for load in loads[:-1]:
        load.wait()

    def place_of_mean(j, carry):
        for side in range(2):
            member = table_s[side, j]
            table_s[side, j] = jnp.where(member == SPECIES, FIELDS, member)
        return carry

    lax.fori_loop(0, REACT, place_of_mean, 0)
    for matrix, into in ((ymat_v, ymat), (emat_v, emat), (zmat_v, zmat)):
        into[...] = matrix[...].astype(jnp.bfloat16)

    filler = jnp.full((4, CY - REACT), 31.0, jnp.float32)
    members = jnp.concatenate([table_v[...].astype(jnp.float32), filler], axis=1)
    members = jnp.concatenate([members, jnp.zeros((12, CY), jnp.float32)], axis=0)
    column = lax.broadcasted_iota(jnp.int32, (CY, 2 * QROWS), 1)
    column = jnp.where(column >= QROWS, column - QROWS, column)
    reaction = lax.broadcasted_iota(jnp.int32, (CY, 2 * QROWS), 0)
    spread = jnp.where(lax.shift_right_logical(column, 3) == reaction, 1.0, 0.0)
    members = dot(members.astype(jnp.bfloat16), spread.astype(jnp.bfloat16))
    level_z = lax.broadcasted_iota(jnp.int32, (CZ, 2 * QROWS), 0)
    same_z = (lax.broadcasted_iota(jnp.int32, (CZ, 2 * QROWS), 1) & 7) == level_z
    for species in range(0, FIELDS, 2):
        both = []
        for at in (species, species + 1):
            total = jnp.zeros((1, 2 * QROWS), jnp.float32)
            if at < SPECIES:
                for which, sign in ((0, -1.0), (1, -1.0), (2, 1.0), (3, 1.0)):
                    total = total + jnp.where(members[which : which + 1] == at, sign, 0.0)
            both.append(jnp.where(same_z, total, 0.0))
        rows = slice(CZ * species, CZ * species + 2 * CZ)
        nuk[rows, :] = jnp.concatenate(both, axis=0).astype(jnp.bfloat16)
    filled = (REACT + 1) * CZ
    for begin in (filled, QROWS + filled):
        qbuf[begin : begin + QROWS - filled, :] = jnp.zeros((QROWS - filled, LANES), jnp.bfloat16)

    lane_block = lax.broadcasted_iota(jnp.int32, (CZ, CY), 1) // 8
    lane = lax.broadcasted_iota(jnp.int32, (CZ, CY), 1)
    at_edge = jnp.logical_or(lane < 4, lane >= CY - 4)
    for quad in range(QUADS):
        packed = jnp.zeros((CZ, CY), jnp.float32)
        for slab in range(min(QUAD, FIELDS - QUAD * quad)):
            packed = jnp.where(
                lane_block // CX == slab, kappas[0, QUAD * quad + slab], packed
            )
        kpack[quad] = packed * (1.0 / SECOND_SCALE)

    @pl.when(moves)
    def _():
        for chunk in chunks:
            placed(0, chunk)
            start(x_copies(0, chunk))

    def z_copy(k, state, chunk):
        begin, end = CHUNKS[chunk]
        return remote(
            state.at[begin:end], zhalo.at[k, begin:end], z_send.at[k, chunk], z_recv.at[k, chunk],
            z_partner,
        )

    def y_copy(k):
        return remote(ypack.at[k], yhalo.at[k], y_send.at[k], y_recv.at[k], y_partner)

    def pack(columns):
        packed = jnp.zeros((CZ, CY), jnp.float32)
        for at, value in enumerate(columns):
            packed = jnp.where(lane_block == at, pltpu.roll(value, (8 * at + 4) % CY, 1), packed)
        return packed

    def send_borders(k, state, chunk):
        z_copy(k, state, chunk).start()
        begin, end = CHUNKS[chunk]
        for first in range(begin, end, QUAD):
            fields = range(first, min(first + QUAD, end))
            ypack[k, first // QUAD] = pack([state[f, x] for f in fields for x in range(CX)])
        if end == FIELDS:
            y_copy(k).start()

    def reactions(state):
        total = state[0]
        for species in range(1, SPECIES):
            total = total + state[species]
        state[FIELDS] = total * (1.0 / SPECIES)
        inverse = 1.0 / state[SPECIES]

        def two(pair, carry):
            both = []
            for at in range(2):
                j = jnp.minimum(2 * pair + at, REACT - 1)
                first, second = table_s[0, j], table_s[1, j]
                speed = jnp.exp(logs[0, j] - barriers[0, j] * inverse)
                both.append(speed * state[first] * state[second])
            begin = pl.multiple_of(16 * pair, 16)
            for x in range(CX):
                high, low = split(jnp.concatenate([both[0][x], both[1][x]], axis=0))
                lanes = slice(CY * x, CY * x + CY)
                qbuf[pl.ds(begin, 16), lanes] = high
                qbuf[pl.ds(QROWS + begin, 16), lanes] = low
            return carry

        lax.fori_loop(0, (REACT + 1) // 2, two, 0, unroll=4)

    def in_parts(source, into):
        for f in range(0, FIELDS, 2):
            for x in range(CX):
                rows = slice(ROWS * x + CZ * f, ROWS * x + CZ * f + 16)
                value = jnp.concatenate([source[f, x], source[f + 1, x]], axis=0)
                into[rows, 0:CY], into[rows, CY:] = split(value)

    def transport(k, state, finish, done=None):
        made[...] = dot(nuk[...], qbuf[...]).reshape(FIELDS, CZ, LANES)
        in_parts(state, parts)
        for chunk in chunks:
            z_copy(k, state, chunk).wait_recv()
        dy[...] = dot(parts[...], ymat[...]).reshape(CX, FIELDS, CZ, 2 * CY)
        in_parts(zhalo.at[k], near)
        for first in (0, 4, 8, 12, 14):
            for x in range(0, CX, 2):
                sides = []
                for at in (x, x + 1):
                    rows = slice(ROWS * at + CZ * first, ROWS * at + CZ * (first + QUAD))
                    sides.append(jnp.concatenate(
                        [parts[rows, 0:CY], near[rows, 0:CY], parts[rows, CY:], near[rows, CY:]],
                        axis=0,
                    ))
                out = dot(zmat[...], jnp.concatenate(sides, axis=1))
                lanes = slice(CY * x, CY * x + 2 * CY)
                dz1[first : first + QUAD, :, lanes] = out[: QUAD * CZ].reshape(QUAD, CZ, 2 * CY)
                dz2[first : first + QUAD, :, lanes] = out[QUAD * CZ :].reshape(QUAD, CZ, 2 * CY)
        y_copy(k).wait_recv()
        value = jnp.concatenate(
            [yhalo[k].reshape(QUADS * CZ, CY), jnp.zeros((CZ, CY), jnp.float32)], axis=0
        )
        out = dot(jnp.concatenate(split(value), axis=1), emat[...])
        for quad in range(QUADS):
            part = out[CZ * quad : CZ * quad + CZ]
            edge[quad] = kpack[quad] * part[:, CY:] - vpack[...] * part[:, 0:CY]

        def one(f, x, packed, at, source):
            values = [state[f, q] for q in range(CX)]
            grad, curv = None, (3.0 * center_coeff) * values[x]
            for q in range(CX):
                if q != x:
                    first, second = weight(q - x)
                    curv = curv + second * values[q]
                    grad = first * values[q] if grad is None else grad + first * values[q]
            lanes = slice(CY * x, CY * x + CY)
            curv = curv + (1.0 / SECOND_SCALE) * (dy[x, f, :, CY:] + dz2[f, :, lanes])
            along = vel[0, x] * grad + vel[1, x] * dy[x, f, :, 0:CY] + vel[2, x] * dz1[f, :, lanes]
            border = pltpu.roll(packed, (CY - (8 * at + 4)) % CY, 1)
            source = source + jnp.where(at_edge, border, 0.0)
            finish(f, x, kappas[0, f] * curv - along + source)

        def quad_of_fields(quad, release, fields=QUAD):
            release = list(release)
            packed = edge[quad]
            for slab in range(fields):
                f = QUAD * quad + slab
                for x in range(CX):
                    at = slab * CX + x
                    if slab == 1 and fields == 2:
                        one(f, x, packed, at, release[x])
                        continue
                    source = made[f, :, CY * x : CY * x + CY]
                    release[x] = release[x] + heats[0, f] * source
                    one(f, x, packed, at, source)
            return tuple(release)

        release = (jnp.zeros((CZ, CY), jnp.float32),) * CX
        if done is None:
            release = lax.fori_loop(0, QUADS - 1, quad_of_fields, release)
            quad_of_fields(QUADS - 1, release, fields=2)
            return
        for chunk, (begin, end) in enumerate(CHUNKS):
            release = lax.fori_loop(begin // QUAD, end // QUAD, quad_of_fields, release)
            if end == FIELDS:
                quad_of_fields(QUADS - 1, release, fields=2)
            done(chunk)

    def x_halo(level, make, done):
        def one(f, carry):
            before = [xhalo[level, 0, f, q] for q in range(CX)]
            after = [xhalo[level, 1, f, q] for q in range(CX)]
            for x in range(CX):
                grad = curv = None
                for q in range(CX):
                    for value, distance in ((before[q], q - 4 - x), (after[q], q + 4 - x)):
                        first, second = weight(distance)
                        if second == 0.0:
                            continue
                        grad = first * value if grad is None else grad + first * value
                        curv = second * value if curv is None else curv + second * value
                make(f, x, kappas[0, f] * curv - vel[0, x] * grad)
            return carry

        for chunk in chunks:
            for copy in x_copies(level, chunk):
                copy.wait_recv()
            lax.fori_loop(*CHUNKS[chunk], one, 0, unroll=4 if chunk < 2 else 2)
            done(chunk)

    def keep(f, x, value):
        local[f, x] = value

    for chunk in chunks:
        placed(2, chunk)
        send_borders(0, lev_c, chunk)

    @pl.when(stays)
    def _():
        for level in (1, 2):
            for chunk in chunks:
                start(x_copies(level, chunk, past.at[level]))

    reactions(lev_c)

    vel_own.wait()
    for x in range(CX):
        vel[1, x] = vel[1, x] * (1.0 / FIRST_SCALE)
        vel[2, x] = vel[2, x] * (1.0 / FIRST_SCALE)
    vpack[...] = pack([vel[1, x] for x in range(CX)] * QUAD)
    transport(0, lev_c, keep)

    @pl.when(moves)
    def _():
        for chunk in chunks:
            placed(1, chunk)
            start(x_copies(1, chunk))
        for chunk in chunks:
            start(x_copies(2, chunk))

    def make(f, x, share):
        xterm[0, f, x] = share
        value = local[f, x] + share
        rate[f, x] = value
        state1[f, x] = lev_c[f, x] + time_step * value

    x_halo(0, make, lambda chunk: send_borders(1, state1, chunk))

    reactions(state1)
    transport(1, state1, keep)

    def make(f, x, share):
        xterm[1, f, x] = share
        value = local[f, x] + 2.0 * xterm[0, f, x] - share
        state2[f, x] = lev_c[f, x] + 0.5 * time_step * (rate[f, x] + value)

    x_halo(1, make, lambda chunk: send_borders(2, state2, chunk))

    reactions(state2)
    transport(2, state2, keep)

    def make(f, x, late):
        before = xterm[1, f, x]
        value = local[f, x] + 2.0 * late - before
        state3[f, x] = state2[f, x] + time_step * value
        rate[f, x] = value + 3.0 * late - 2.0 * before

    x_halo(2, make, lambda chunk: send_borders(3, state3, chunk))

    reactions(state3)

    def last(f, x, value):
        result[f, x] = state2[f, x] + 0.5 * time_step * (rate[f, x] + value)

    def outs(chunk):
        begin, end = CHUNKS[chunk]
        return result.at[begin:end], next_out.at[begin:end]

    def out_swap(chunk):
        src, dst = outs(chunk)
        return remote(src, dst, o_send.at[chunk], o_recv.at[chunk], opposite)

    def out_own(chunk):
        src, dst = outs(chunk)
        return pltpu.make_async_copy(src, dst, o_recv.at[chunk])

    def done(chunk):
        @pl.when(moves)
        def _():
            out_swap(chunk).start()

        @pl.when(stays)
        def _():
            out_own(chunk).start()

    transport(3, state3, last, done)

    for level in range(3):
        for chunk in chunks:
            for copy in x_copies(level, chunk):
                copy.wait_send()
    for k, state in enumerate((lev_c, state1, state2, state3)):
        for chunk in chunks:
            z_copy(k, state, chunk).wait_send()
        y_copy(k).wait_send()

    @pl.when(moves)
    def _():
        vel_swap.wait_send()
        for chunk in chunks:
            for copy in [swap(level, chunk) for level in range(3)] + [out_swap(chunk)]:
                copy.wait_send()

    for chunk in chunks:
        out_own(chunk).wait()


def hand_out(next_ref, conc_out, therm_out, sem):
    copies = [
        pltpu.make_async_copy(next_ref.at[0:SPECIES], conc_out, sem.at[0]),
        pltpu.make_async_copy(next_ref.at[SPECIES], therm_out, sem.at[1]),
    ]
    for copy in copies:
        copy.start()
    for copy in copies:
        copy.wait()


def local(
    concentration_levels,
    thermal_levels,
    fluid_velocity,
    diffusivity,
    natural_logged_prefactors,
    energy_barrier_kelvin,
    enthalpy_yield_per_mole,
    stoichiometric_member_table,
):
    n_gx = lax.axis_size("gx")
    any_space = pl.BlockSpec(memory_space=pl.ANY)
    f32, bf16 = jnp.float32, jnp.bfloat16
    block = (FIELDS, CX, CZ, CY)
    wide = (FIELDS + 1, CX, CZ, CY)
    parts = len(CHUNKS)
    dma = pltpu.SemaphoreType.DMA
    scratch = [
        pltpu.VMEM((3,) + block, f32),
        pltpu.VMEM(block, f32),
        pltpu.VMEM(block, f32),
        pltpu.VMEM(wide, f32),
        pltpu.VMEM((3, CX, CZ, CY), f32),
        pltpu.VMEM((3, 2) + block, f32),
        pltpu.VMEM((2,) + block, f32),
        pltpu.VMEM(wide, f32),
        pltpu.VMEM(wide, f32),
        pltpu.VMEM(wide, f32),
        pltpu.VMEM((4,) + block, f32),
        pltpu.VMEM((4, QUADS, CZ, CY), f32),
        pltpu.VMEM((4, QUADS, CZ, CY), f32),
        pltpu.VMEM(block, f32),
        pltpu.VMEM(block, f32),
        pltpu.VMEM(block, f32),
        pltpu.VMEM((2 * QROWS, LANES), bf16),
        pltpu.VMEM((FIELDS, CZ, LANES), f32),
        pltpu.VMEM((CX * ROWS, 2 * CY), bf16),
        pltpu.VMEM((CX * ROWS, 2 * CY), bf16),
        pltpu.VMEM((CX, FIELDS, CZ, 2 * CY), f32),
        pltpu.VMEM((FIELDS, CZ, LANES), f32),
        pltpu.VMEM((FIELDS, CZ, LANES), f32),
        pltpu.VMEM((QUADS, CZ, CY), f32),
        pltpu.VMEM((QUADS, CZ, CY), f32),
        pltpu.VMEM((CZ, CY), f32),
        pltpu.VMEM((ROWS, 2 * QROWS), bf16),
        pltpu.VMEM((2 * CY, 2 * CY), bf16),
        pltpu.VMEM((2 * CY, 2 * CY), bf16),
        pltpu.VMEM((2 * QUAD * CZ, 4 * QUAD * CZ), bf16),
        pltpu.VMEM((2 * CY, 2 * CY), f32),
        pltpu.VMEM((2 * CY, 2 * CY), f32),
        pltpu.VMEM((2 * QUAD * CZ, 4 * QUAD * CZ), f32),
        pltpu.SMEM((4, REACT), jnp.int32),
        pltpu.SMEM((1, REACT), f32),
        pltpu.SMEM((1, REACT), f32),
        pltpu.SMEM((1, SPECIES), f32),
        pltpu.SMEM((1, FIELDS), f32),
        pltpu.VMEM((4, REACT), jnp.int32),
        pltpu.VMEM((3, CX, CZ, CY), f32),
        dma((parts, 2)),
        dma((10,)),
        dma((2,)),
        dma((3, parts)),
        dma((3, parts)),
        dma((3, 2, parts)),
        dma((3, 2, parts)),
        dma((4, parts)),
        dma((4, parts)),
        dma((4,)),
        dma((4,)),
        dma((parts,)),
        dma((parts,)),
    ]
    stepped = pl.pallas_call(
        functools.partial(kernel, n_gx),
        out_shape=pltpu.VMEM(block, f32),
        in_specs=[any_space] * 11,
        out_specs=any_space,
        scratch_shapes=scratch,
        compiler_params=pltpu.CompilerParams(
            collective_id=0, has_side_effects=True, vmem_limit_bytes=40 * 1024 * 1024
        ),
    )(*[pltpu.with_memory_space_constraint(value, pltpu.HBM) for value in (
        concentration_levels,
        thermal_levels,
        fluid_velocity,
        stoichiometric_member_table,
        natural_logged_prefactors[None],
        energy_barrier_kelvin[None],
        enthalpy_yield_per_mole[None],
        diffusivity[None],
        jnp.asarray(y_matrix()),
        jnp.asarray(edge_matrix()),
        jnp.asarray(z_matrix()),
    )])
    return pl.pallas_call(
        hand_out,
        out_shape=(
            jax.ShapeDtypeStruct((SPECIES, CX, CZ, CY), f32),
            jax.ShapeDtypeStruct((CX, CZ, CY), f32),
        ),
        in_specs=[any_space],
        out_specs=(any_space, any_space),
        scratch_shapes=[dma((2,))],
        compiler_params=pltpu.CompilerParams(vmem_limit_bytes=8 * 1024 * 1024),
    )(stepped)


def solution(mesh):
    in_specs = (
        P(None, None, "gx", "gz", "gy"),
        P(None, "gx", "gz", "gy"),
        P(None, "gx", "gz", "gy"),
        P(),
        P(),
        P(),
        P(),
        P(),
    )
    out_specs = (P(None, "gx", "gz", "gy"), P("gx", "gz", "gy"))
    return jax.shard_map(local, mesh=mesh, in_specs=in_specs, out_specs=out_specs, check_vma=False)
```

```python
import functools

import jax
import jax.numpy as jnp
import numpy as np
from jax import lax
from jax.experimental import pallas as pl
from jax.experimental.pallas import tpu as pltpu
from jax.sharding import PartitionSpec as P

SPECIES = 17
FIELDS = 18
REACT = 73
CX = 4
CZ = 8
CY = 128
ROWS = FIELDS * CZ
LANES = CX * CY
QUAD = 4
QUADS = (FIELDS + QUAD - 1) // QUAD
QROWS = 640
CHUNKS = ((0, 8), (8, 16), (16, 18))
BESIDE = (1,)

time_step = 0.125
first_coeffs = (4.0 / 5.0, -1.0 / 5.0, 4.0 / 105.0, -1.0 / 280.0)
second_coeffs = (8.0 / 5.0, -1.0 / 5.0, 8.0 / 315.0, -1.0 / 560.0)
center_coeff = -205.0 / 72.0

MESH = pl.DeviceIdType.MESH


FIRST_SCALE = 840.0
SECOND_SCALE = 5040.0
first_scaled = (672.0, -168.0, 32.0, -3.0)
second_scaled = (8064.0, -1008.0, 128.0, -9.0)


def weight(distance):
    size = abs(distance)
    if size == 0 or size > 4:
        return 0.0, 0.0
    sign = 1.0 if distance > 0 else -1.0
    return sign * first_coeffs[size - 1], second_coeffs[size - 1]


def scaled(distance):
    size = abs(distance)
    if size == 0 or size > 4:
        return 0.0, 0.0
    sign = 1.0 if distance > 0 else -1.0
    return sign * first_scaled[size - 1], second_scaled[size - 1]


def y_matrix():
    matrix = np.zeros((CY, 2 * CY), np.float32)
    for out in range(CY):
        for at in range(CY):
            matrix[at, out], matrix[at, CY + out] = scaled(at - out)
    return np.concatenate([matrix, matrix])


def edge_matrix():
    matrix = np.zeros((CY, 2 * CY), np.float32)
    for base in range(0, CY, 8):
        for at in range(8):
            for out in range(8):
                if (at < 4) != (out < 4):
                    first, second = scaled(at - out)
                    matrix[base + at, base + out] = first
                    matrix[base + at, CY + base + out] = second
    return np.concatenate([matrix, matrix])


def z_matrix():
    half = QUAD * CZ
    matrix = np.zeros((2 * half, 2 * half), np.float32)
    for slab in range(QUAD):
        for out in range(CZ):
            for step in range(-4, 5):
                at = out + step
                column = slab * CZ + at % CZ + (0 if 0 <= at < CZ else half)
                first, second = scaled(step)
                matrix[slab * CZ + out, column] += first
                matrix[half + slab * CZ + out, column] += second
    return np.concatenate([matrix, matrix], axis=1)


def split(value):
    high = value.astype(jnp.bfloat16)
    return high, (value - high.astype(jnp.float32)).astype(jnp.bfloat16)


def dot(left, right):
    return jnp.dot(left, right, preferred_element_type=jnp.float32)


def kernel(
    n_gx,
    conc, therm, veloc, table_h, logs_h, barriers_h, heats_h, kappas_h, ymat_h, emat_h, zmat_h,
    next_out,
    past, lev_a, lev_n, lev_c, vel, xhalo, xterm, state1, state2, state3, zhalo, ypack, yhalo,
    rate, local, result, qbuf, made, parts, near, dy, dz1, dz2, edge, kpack, vpack, nuk,
    ymat, emat, zmat, ymat_v, emat_v, zmat_v,
    table_s, logs, barriers, heats, kappas, table_v,
    vel_near, relay, hop_send, hop_recv, on_send, past_sem, ld_sem, vel_send, swap_send, arrive, x_send, x_recv, z_send, z_recv, y_send, y_recv,
    o_send, o_recv,
):
    gx, gy, gz = lax.axis_index("gx"), lax.axis_index("gy"), lax.axis_index("gz")
    period = max(n_gx // 8, 1)

    def half_of(at):
        return lax.rem(lax.div(at, period), 2)

    mirrored = half_of(gx)
    moves = lax.rem(gy + gz + mirrored, 2) == 1

    def x_beside(at):
        flips = half_of(at) != mirrored
        return {
            "gx": at,
            "gy": jnp.where(flips, 1 - gy, gy),
            "gz": jnp.where(flips, 1 - gz, gz),
        }

    right = x_beside(lax.rem(gx + 1, n_gx))
    left = x_beside(lax.rem(gx + n_gx - 1, n_gx))
    z_partner = {"gx": gx, "gy": 1 - gy, "gz": gz}
    y_partner = {"gx": gx, "gy": gy, "gz": 1 - gz}
    opposite = {"gx": gx, "gy": 1 - gy, "gz": 1 - gz}

    def remote(src, dst, send, recv, where):
        return pltpu.make_async_remote_copy(
            src_ref=src, dst_ref=dst, send_sem=send, recv_sem=recv,
            device_id=where, device_id_type=MESH,
        )

    past_loads = []
    for chunk, (begin, end) in enumerate(CHUNKS):
        stop = min(end, SPECIES)
        copies = [(conc.at[:, begin:stop], past.at[:, begin:stop])]
        if end == FIELDS:
            copies.append((therm, past.at[:, SPECIES]))
        past_loads.append([
            pltpu.make_async_copy(src, dst, past_sem.at[chunk, at])
            for at, (src, dst) in enumerate(copies)
        ])
    shared = ((table_h, table_v), (ymat_h, ymat_v), (emat_h, emat_v), (zmat_h, zmat_v), (table_h, table_s),
              (logs_h, logs), (barriers_h, barriers), (heats_h, heats), (kappas_h, kappas),
              (veloc, vel_near))
    loads = [
        pltpu.make_async_copy(src, dst, ld_sem.at[at]) for at, (src, dst) in enumerate(shared)
    ]
    for copy in [copy for copies in past_loads for copy in copies] + loads:
        copy.start()

    barrier = pltpu.get_barrier_semaphore()
    for where in (left, right, z_partner, y_partner, opposite):
        pl.semaphore_signal(barrier, inc=1, device_id=where, device_id_type=MESH)

    def moved(level, chunk):
        begin, end = CHUNKS[chunk]
        return past.at[level, begin:end], (lev_a, lev_n, lev_c)[level].at[begin:end]

    def swap(level, chunk):
        src, dst = moved(level, chunk)
        return remote(src, dst, swap_send.at[level, chunk], arrive.at[level, chunk], opposite)

    def hop(chunk):
        span = slice(*CHUNKS[chunk])
        return remote(
            past.at[2, span], relay.at[0, span], hop_send.at[chunk], hop_recv.at[0, chunk],
            z_partner,
        )

    def on(chunk):
        span = slice(*CHUNKS[chunk])
        return remote(
            relay.at[0, span], lev_c.at[span], on_send.at[0, chunk], arrive.at[2, chunk], y_partner
        )

    def own(level, chunk):
        src, dst = moved(level, chunk)
        return pltpu.make_async_copy(src, dst, arrive.at[level, chunk])

    def placed(level, chunk):
        src, dst = moved(level, chunk)
        pltpu.make_async_copy(dst, dst, arrive.at[level, chunk]).wait()

    vel_swap = remote(vel_near, vel, vel_send.at[0], vel_send.at[1], opposite)
    vel_own = pltpu.make_async_copy(vel_near, vel, vel_send.at[1])

    levels = (lev_a, lev_n, lev_c)

    def x_copies(level, chunk, source=None):
        begin, end = CHUNKS[chunk]
        src = (levels[level] if source is None else source).at[begin:end]
        return [
            remote(
                src, xhalo.at[level, side, begin:end],
                x_send.at[level, side, chunk], x_recv.at[level, side, chunk], where,
            )
            for side, where in ((0, right), (1, left))
        ]

    def delay(chunk):
        for copy in past_loads[chunk]:
            copy.wait()

        def one(field, carry):
            past[0, field] = 2.0 * past[1, field] - past[0, field]
            return carry

        lax.fori_loop(*CHUNKS[chunk], one, 0, unroll=2)

    def start(copies):
        for copy in copies:
            copy.start()

    stays = jnp.logical_not(moves)
    chunks = range(len(CHUNKS))

    for chunk in chunks:
        delay(chunk)
    loads[-1].wait()
    pl.semaphore_wait(barrier, 5)

    @pl.when(stays)
    def _():
        vel_own.start()
        for chunk in chunks:
            own(2, chunk).start()
        for chunk in chunks:
            start(x_copies(0, chunk, past.at[0]))

    @pl.when(moves)
    def _():
        for chunk in chunks:
            hop(chunk).start()
            swap(0, chunk).start()
        vel_swap.start()
        for chunk in chunks:
            swap(1, chunk).start()

    for load in loads[:-1]:
        load.wait()

    def place_of_mean(j, carry):
        for side in range(2):
            member = table_s[side, j]
            table_s[side, j] = jnp.where(member == SPECIES, FIELDS, member)
        return carry

    lax.fori_loop(0, REACT, place_of_mean, 0)
    for matrix, into in ((ymat_v, ymat), (emat_v, emat), (zmat_v, zmat)):
        into[...] = matrix[...].astype(jnp.bfloat16)

    filler = jnp.full((4, CY - REACT), 31.0, jnp.float32)
    members = jnp.concatenate([table_v[...].astype(jnp.float32), filler], axis=1)
    members = jnp.concatenate([members, jnp.zeros((12, CY), jnp.float32)], axis=0)
    column = lax.broadcasted_iota(jnp.int32, (CY, 2 * QROWS), 1)
    column = jnp.where(column >= QROWS, column - QROWS, column)
    reaction = lax.broadcasted_iota(jnp.int32, (CY, 2 * QROWS), 0)
    spread = jnp.where(lax.shift_right_logical(column, 3) == reaction, 1.0, 0.0)
    members = dot(members.astype(jnp.bfloat16), spread.astype(jnp.bfloat16))
    level_z = lax.broadcasted_iota(jnp.int32, (CZ, 2 * QROWS), 0)
    same_z = (lax.broadcasted_iota(jnp.int32, (CZ, 2 * QROWS), 1) & 7) == level_z
    for species in range(0, FIELDS, 2):
        both = []
        for at in (species, species + 1):
            total = jnp.zeros((1, 2 * QROWS), jnp.float32)
            if at < SPECIES:
                for which, sign in ((0, -1.0), (1, -1.0), (2, 1.0), (3, 1.0)):
                    total = total + jnp.where(members[which : which + 1] == at, sign, 0.0)
            both.append(jnp.where(same_z, total, 0.0))
        rows = slice(CZ * species, CZ * species + 2 * CZ)
        nuk[rows, :] = jnp.concatenate(both, axis=0).astype(jnp.bfloat16)
    filled = (REACT + 1) * CZ
    for begin in (filled, QROWS + filled):
        qbuf[begin : begin + QROWS - filled, :] = jnp.zeros((QROWS - filled, LANES), jnp.bfloat16)

    lane_block = lax.broadcasted_iota(jnp.int32, (CZ, CY), 1) // 8
    lane = lax.broadcasted_iota(jnp.int32, (CZ, CY), 1)
    at_edge = jnp.logical_or(lane < 4, lane >= CY - 4)
    for quad in range(QUADS):
        packed = jnp.zeros((CZ, CY), jnp.float32)
        for slab in range(min(QUAD, FIELDS - QUAD * quad)):
            packed = jnp.where(
                lane_block // CX == slab, kappas[0, QUAD * quad + slab], packed
            )
        kpack[quad] = packed * (1.0 / SECOND_SCALE)

    @pl.when(moves)
    def _():
        for chunk in chunks:
            placed(0, chunk)
            start(x_copies(0, chunk))

    def z_copy(k, state, chunk):
        begin, end = CHUNKS[chunk]
        return remote(
            state.at[begin:end], zhalo.at[k, begin:end], z_send.at[k, chunk], z_recv.at[k, chunk],
            z_partner,
        )

    def y_copy(k):
        return remote(ypack.at[k], yhalo.at[k], y_send.at[k], y_recv.at[k], y_partner)

    def pack(columns):
        packed = jnp.zeros((CZ, CY), jnp.float32)
        for at, value in enumerate(columns):
            packed = jnp.where(lane_block == at, pltpu.roll(value, (8 * at + 4) % CY, 1), packed)
        return packed

    def send_borders(k, state, chunk):
        z_copy(k, state, chunk).start()
        begin, end = CHUNKS[chunk]
        for first in range(begin, end, QUAD):
            fields = range(first, min(first + QUAD, end))
            ypack[k, first // QUAD] = pack([state[f, x] for f in fields for x in range(CX)])
        if end == FIELDS:
            y_copy(k).start()

    def reactions(state):
        total = state[0]
        for species in range(1, SPECIES):
            total = total + state[species]
        state[FIELDS] = total * (1.0 / SPECIES)
        inverse = 1.0 / state[SPECIES]

        def two(pair, carry):
            both = []
            for at in range(2):
                j = jnp.minimum(2 * pair + at, REACT - 1)
                first, second = table_s[0, j], table_s[1, j]
                speed = jnp.exp(logs[0, j] - barriers[0, j] * inverse)
                both.append(speed * state[first] * state[second])
            begin = pl.multiple_of(16 * pair, 16)
            for x in range(CX):
                high, low = split(jnp.concatenate([both[0][x], both[1][x]], axis=0))
                lanes = slice(CY * x, CY * x + CY)
                qbuf[pl.ds(begin, 16), lanes] = high
                qbuf[pl.ds(QROWS + begin, 16), lanes] = low
            return carry

        lax.fori_loop(0, (REACT + 1) // 2, two, 0, unroll=4)

    def in_parts(source, into):
        for f in range(0, FIELDS, 2):
            for x in range(CX):
                rows = slice(ROWS * x + CZ * f, ROWS * x + CZ * f + 16)
                value = jnp.concatenate([source[f, x], source[f + 1, x]], axis=0)
                into[rows, 0:CY], into[rows, CY:] = split(value)

    def transport(k, state, finish, done=None):
        made[...] = dot(nuk[...], qbuf[...]).reshape(FIELDS, CZ, LANES)
        in_parts(state, parts)
        for chunk in chunks:
            z_copy(k, state, chunk).wait_recv()
        dy[...] = dot(parts[...], ymat[...]).reshape(CX, FIELDS, CZ, 2 * CY)
        in_parts(zhalo.at[k], near)
        for first in (0, 4, 8, 12, 14):
            for x in range(0, CX, 2):
                sides = []
                for at in (x, x + 1):
                    rows = slice(ROWS * at + CZ * first, ROWS * at + CZ * (first + QUAD))
                    sides.append(jnp.concatenate(
                        [parts[rows, 0:CY], near[rows, 0:CY], parts[rows, CY:], near[rows, CY:]],
                        axis=0,
                    ))
                out = dot(zmat[...], jnp.concatenate(sides, axis=1))
                lanes = slice(CY * x, CY * x + 2 * CY)
                dz1[first : first + QUAD, :, lanes] = out[: QUAD * CZ].reshape(QUAD, CZ, 2 * CY)
                dz2[first : first + QUAD, :, lanes] = out[QUAD * CZ :].reshape(QUAD, CZ, 2 * CY)
        y_copy(k).wait_recv()
        value = jnp.concatenate(
            [yhalo[k].reshape(QUADS * CZ, CY), jnp.zeros((CZ, CY), jnp.float32)], axis=0
        )
        out = dot(jnp.concatenate(split(value), axis=1), emat[...])
        for quad in range(QUADS):
            part = out[CZ * quad : CZ * quad + CZ]
            edge[quad] = kpack[quad] * part[:, CY:] - vpack[...] * part[:, 0:CY]

        def one(f, x, packed, at, source):
            values = [state[f, q] for q in range(CX)]
            grad, curv = None, (3.0 * center_coeff) * values[x]
            for q in range(CX):
                if q != x:
                    first, second = weight(q - x)
                    curv = curv + second * values[q]
                    grad = first * values[q] if grad is None else grad + first * values[q]
            lanes = slice(CY * x, CY * x + CY)
            curv = curv + (1.0 / SECOND_SCALE) * (dy[x, f, :, CY:] + dz2[f, :, lanes])
            along = vel[0, x] * grad + vel[1, x] * dy[x, f, :, 0:CY] + vel[2, x] * dz1[f, :, lanes]
            border = pltpu.roll(packed, (CY - (8 * at + 4)) % CY, 1)
            source = source + jnp.where(at_edge, border, 0.0)
            finish(f, x, kappas[0, f] * curv - along + source)

        def quad_of_fields(quad, release, fields=QUAD):
            release = list(release)
            packed = edge[quad]
            for slab in range(fields):
                f = QUAD * quad + slab
                for x in range(CX):
                    at = slab * CX + x
                    if slab == 1 and fields == 2:
                        one(f, x, packed, at, release[x])
                        continue
                    source = made[f, :, CY * x : CY * x + CY]
                    release[x] = release[x] + heats[0, f] * source
                    one(f, x, packed, at, source)
            return tuple(release)

        release = (jnp.zeros((CZ, CY), jnp.float32),) * CX
        if done is None:
            release = lax.fori_loop(0, QUADS - 1, quad_of_fields, release)
            quad_of_fields(QUADS - 1, release, fields=2)
            return
        for chunk, (begin, end) in enumerate(CHUNKS):
            release = lax.fori_loop(begin // QUAD, end // QUAD, quad_of_fields, release)
            if end == FIELDS:
                quad_of_fields(QUADS - 1, release, fields=2)
            done(chunk)

    def x_halo(level, make, done):
        def one(f, carry):
            before = [xhalo[level, 0, f, q] for q in range(CX)]
            after = [xhalo[level, 1, f, q] for q in range(CX)]
            for x in range(CX):
                grad = curv = None
                for q in range(CX):
                    for value, distance in ((before[q], q - 4 - x), (after[q], q + 4 - x)):
                        first, second = weight(distance)
                        if second == 0.0:
                            continue
                        grad = first * value if grad is None else grad + first * value
                        curv = second * value if curv is None else curv + second * value
                make(f, x, kappas[0, f] * curv - vel[0, x] * grad)
            return carry

        for chunk in chunks:
            for copy in x_copies(level, chunk):
                copy.wait_recv()
            lax.fori_loop(*CHUNKS[chunk], one, 0, unroll=4 if chunk < 2 else 2)
            done(chunk)

    def keep(f, x, value):
        local[f, x] = value

    @pl.when(stays)
    def _():
        for chunk in chunks:
            hop(chunk).wait_recv()
            on(chunk).start()

    for chunk in chunks:
        placed(2, chunk)
        send_borders(0, lev_c, chunk)

    @pl.when(stays)
    def _():
        for level in (1, 2):
            for chunk in chunks:
                start(x_copies(level, chunk, past.at[level]))

    reactions(lev_c)

    @pl.when(moves)
    def _():
        placed(1, 0)
        start(x_copies(1, 0))


    vel_own.wait()
    for x in range(CX):
        vel[1, x] = vel[1, x] * (1.0 / FIRST_SCALE)
        vel[2, x] = vel[2, x] * (1.0 / FIRST_SCALE)
    vpack[...] = pack([vel[1, x] for x in range(CX)] * QUAD)
    transport(0, lev_c, keep)

    @pl.when(moves)
    def _():
        for chunk in chunks[1:]:
            placed(1, chunk)
            start(x_copies(1, chunk))
        for chunk in chunks:
            start(x_copies(2, chunk))

    def make(f, x, share):
        xterm[0, f, x] = share
        value = local[f, x] + share
        rate[f, x] = value
        state1[f, x] = lev_c[f, x] + time_step * value

    x_halo(0, make, lambda chunk: send_borders(1, state1, chunk))

    reactions(state1)
    transport(1, state1, keep)

    def make(f, x, share):
        xterm[1, f, x] = share
        value = local[f, x] + 2.0 * xterm[0, f, x] - share
        state2[f, x] = lev_c[f, x] + 0.5 * time_step * (rate[f, x] + value)

    x_halo(1, make, lambda chunk: send_borders(2, state2, chunk))

    reactions(state2)
    transport(2, state2, keep)

    def make(f, x, late):
        before = xterm[1, f, x]
        value = local[f, x] + 2.0 * late - before
        state3[f, x] = state2[f, x] + time_step * value
        rate[f, x] = value + 3.0 * late - 2.0 * before

    x_halo(2, make, lambda chunk: send_borders(3, state3, chunk))

    reactions(state3)

    def last(f, x, value):
        result[f, x] = state2[f, x] + 0.5 * time_step * (rate[f, x] + value)

    def outs(chunk):
        begin, end = CHUNKS[chunk]
        return result.at[begin:end], next_out.at[begin:end]

    def out_swap(chunk):
        src, dst = outs(chunk)
        where, recv = opposite, o_recv.at[chunk]
        if chunk in BESIDE:
            dst, where, recv = relay.at[1, slice(*CHUNKS[chunk])], z_partner, hop_recv.at[1, chunk]
        return remote(src, dst, o_send.at[chunk], recv, where)

    def out_on(chunk):
        span = slice(*CHUNKS[chunk])
        return remote(
            relay.at[1, span], next_out.at[span], on_send.at[1, chunk], o_recv.at[chunk], y_partner
        )

    def out_own(chunk):
        src, dst = outs(chunk)
        return pltpu.make_async_copy(src, dst, o_recv.at[chunk])

    def done(chunk):
        @pl.when(moves)
        def _():
            out_swap(chunk).start()

        @pl.when(stays)
        def _():
            out_own(chunk).start()

    transport(3, state3, last, done)

    @pl.when(stays)
    def _():
        for chunk in BESIDE:
            out_swap(chunk).wait_recv()
            out_on(chunk).start()

    for level in range(3):
        for chunk in chunks:
            for copy in x_copies(level, chunk):
                copy.wait_send()
    for k, state in enumerate((lev_c, state1, state2, state3)):
        for chunk in chunks:
            z_copy(k, state, chunk).wait_send()
        y_copy(k).wait_send()

    @pl.when(moves)
    def _():
        vel_swap.wait_send()
        for chunk in chunks:
            for copy in (swap(0, chunk), swap(1, chunk), hop(chunk), out_swap(chunk)):
                copy.wait_send()

    @pl.when(stays)
    def _():
        for chunk in chunks:
            on(chunk).wait_send()
        for chunk in BESIDE:
            out_on(chunk).wait_send()

    for chunk in chunks:
        out_own(chunk).wait()


def hand_out(next_ref, conc_out, therm_out, sem):
    copies = [
        pltpu.make_async_copy(next_ref.at[0:SPECIES], conc_out, sem.at[0]),
        pltpu.make_async_copy(next_ref.at[SPECIES], therm_out, sem.at[1]),
    ]
    for copy in copies:
        copy.start()
    for copy in copies:
        copy.wait()


def local(
    concentration_levels,
    thermal_levels,
    fluid_velocity,
    diffusivity,
    natural_logged_prefactors,
    energy_barrier_kelvin,
    enthalpy_yield_per_mole,
    stoichiometric_member_table,
):
    n_gx = lax.axis_size("gx")
    any_space = pl.BlockSpec(memory_space=pl.ANY)
    f32, bf16 = jnp.float32, jnp.bfloat16
    block = (FIELDS, CX, CZ, CY)
    wide = (FIELDS + 1, CX, CZ, CY)
    parts = len(CHUNKS)
    dma = pltpu.SemaphoreType.DMA
    scratch = [
        pltpu.VMEM((3,) + block, f32),
        pltpu.VMEM(block, f32),
        pltpu.VMEM(block, f32),
        pltpu.VMEM(wide, f32),
        pltpu.VMEM((3, CX, CZ, CY), f32),
        pltpu.VMEM((3, 2) + block, f32),
        pltpu.VMEM((2,) + block, f32),
        pltpu.VMEM(wide, f32),
        pltpu.VMEM(wide, f32),
        pltpu.VMEM(wide, f32),
        pltpu.VMEM((4,) + block, f32),
        pltpu.VMEM((4, QUADS, CZ, CY), f32),
        pltpu.VMEM((4, QUADS, CZ, CY), f32),
        pltpu.VMEM(block, f32),
        pltpu.VMEM(block, f32),
        pltpu.VMEM(block, f32),
        pltpu.VMEM((2 * QROWS, LANES), bf16),
        pltpu.VMEM((FIELDS, CZ, LANES), f32),
        pltpu.VMEM((CX * ROWS, 2 * CY), bf16),
        pltpu.VMEM((CX * ROWS, 2 * CY), bf16),
        pltpu.VMEM((CX, FIELDS, CZ, 2 * CY), f32),
        pltpu.VMEM((FIELDS, CZ, LANES), f32),
        pltpu.VMEM((FIELDS, CZ, LANES), f32),
        pltpu.VMEM((QUADS, CZ, CY), f32),
        pltpu.VMEM((QUADS, CZ, CY), f32),
        pltpu.VMEM((CZ, CY), f32),
        pltpu.VMEM((ROWS, 2 * QROWS), bf16),
        pltpu.VMEM((2 * CY, 2 * CY), bf16),
        pltpu.VMEM((2 * CY, 2 * CY), bf16),
        pltpu.VMEM((2 * QUAD * CZ, 4 * QUAD * CZ), bf16),
        pltpu.VMEM((2 * CY, 2 * CY), f32),
        pltpu.VMEM((2 * CY, 2 * CY), f32),
        pltpu.VMEM((2 * QUAD * CZ, 4 * QUAD * CZ), f32),
        pltpu.SMEM((4, REACT), jnp.int32),
        pltpu.SMEM((1, REACT), f32),
        pltpu.SMEM((1, REACT), f32),
        pltpu.SMEM((1, SPECIES), f32),
        pltpu.SMEM((1, FIELDS), f32),
        pltpu.VMEM((4, REACT), jnp.int32),
        pltpu.VMEM((3, CX, CZ, CY), f32),
        pltpu.VMEM((2,) + block, f32),
        dma((parts,)),
        dma((2, parts)),
        dma((2, parts)),
        dma((parts, 2)),
        dma((10,)),
        dma((2,)),
        dma((3, parts)),
        dma((3, parts)),
        dma((3, 2, parts)),
        dma((3, 2, parts)),
        dma((4, parts)),
        dma((4, parts)),
        dma((4,)),
        dma((4,)),
        dma((parts,)),
        dma((parts,)),
    ]
    stepped = pl.pallas_call(
        functools.partial(kernel, n_gx),
        out_shape=pltpu.VMEM(block, f32),
        in_specs=[any_space] * 11,
        out_specs=any_space,
        scratch_shapes=scratch,
        compiler_params=pltpu.CompilerParams(
            collective_id=0, has_side_effects=True, vmem_limit_bytes=40 * 1024 * 1024
        ),
    )(*[pltpu.with_memory_space_constraint(value, pltpu.HBM) for value in (
        concentration_levels,
        thermal_levels,
        fluid_velocity,
        stoichiometric_member_table,
        natural_logged_prefactors[None],
        energy_barrier_kelvin[None],
        enthalpy_yield_per_mole[None],
        diffusivity[None],
        jnp.asarray(y_matrix()),
        jnp.asarray(edge_matrix()),
        jnp.asarray(z_matrix()),
    )])
    return pl.pallas_call(
        hand_out,
        out_shape=(
            jax.ShapeDtypeStruct((SPECIES, CX, CZ, CY), f32),
            jax.ShapeDtypeStruct((CX, CZ, CY), f32),
        ),
        in_specs=[any_space],
        out_specs=(any_space, any_space),
        scratch_shapes=[dma((2,))],
        compiler_params=pltpu.CompilerParams(vmem_limit_bytes=8 * 1024 * 1024),
    )(stepped)


def solution(mesh):
    in_specs = (
        P(None, None, "gx", "gz", "gy"),
        P(None, "gx", "gz", "gy"),
        P(None, "gx", "gz", "gy"),
        P(),
        P(),
        P(),
        P(),
        P(),
    )
    out_specs = (P(None, "gx", "gz", "gy"), P("gx", "gz", "gy"))
    return jax.shard_map(local, mesh=mesh, in_specs=in_specs, out_specs=out_specs, check_vma=False)
```

```python
import functools

import jax
import jax.numpy as jnp
import numpy as np
from jax import lax
from jax.experimental import pallas as pl
from jax.experimental.pallas import tpu as pltpu
from jax.sharding import PartitionSpec as P

SPECIES = 17
FIELDS = 18
REACT = 73
CX = 4
CZ = 8
CY = 128
ROWS = FIELDS * CZ
LANES = CX * CY
QUAD = 4
QUADS = (FIELDS + QUAD - 1) // QUAD
QROWS = 640
CHUNKS = ((0, 8), (8, 16), (16, 18))
BESIDE = (0,)

time_step = 0.125
first_coeffs = (4.0 / 5.0, -1.0 / 5.0, 4.0 / 105.0, -1.0 / 280.0)
second_coeffs = (8.0 / 5.0, -1.0 / 5.0, 8.0 / 315.0, -1.0 / 560.0)
center_coeff = -205.0 / 72.0

MESH = pl.DeviceIdType.MESH


FIRST_SCALE = 840.0
SECOND_SCALE = 5040.0
first_scaled = (672.0, -168.0, 32.0, -3.0)
second_scaled = (8064.0, -1008.0, 128.0, -9.0)


def weight(distance):
    size = abs(distance)
    if size == 0 or size > 4:
        return 0.0, 0.0
    sign = 1.0 if distance > 0 else -1.0
    return sign * first_coeffs[size - 1], second_coeffs[size - 1]


def scaled(distance):
    size = abs(distance)
    if size == 0 or size > 4:
        return 0.0, 0.0
    sign = 1.0 if distance > 0 else -1.0
    return sign * first_scaled[size - 1], second_scaled[size - 1]


def y_matrix():
    matrix = np.zeros((CY, 2 * CY), np.float32)
    for out in range(CY):
        for at in range(CY):
            matrix[at, out], matrix[at, CY + out] = scaled(at - out)
    return np.concatenate([matrix, matrix])


def edge_matrix():
    matrix = np.zeros((CY, 2 * CY), np.float32)
    for base in range(0, CY, 8):
        for at in range(8):
            for out in range(8):
                if (at < 4) != (out < 4):
                    first, second = scaled(at - out)
                    matrix[base + at, base + out] = first
                    matrix[base + at, CY + base + out] = second
    return np.concatenate([matrix, matrix])


def z_matrix():
    half = QUAD * CZ
    matrix = np.zeros((2 * half, 2 * half), np.float32)
    for slab in range(QUAD):
        for out in range(CZ):
            for step in range(-4, 5):
                at = out + step
                column = slab * CZ + at % CZ + (0 if 0 <= at < CZ else half)
                first, second = scaled(step)
                matrix[slab * CZ + out, column] += first
                matrix[half + slab * CZ + out, column] += second
    return np.concatenate([matrix, matrix], axis=1)


def split(value):
    high = value.astype(jnp.bfloat16)
    return high, (value - high.astype(jnp.float32)).astype(jnp.bfloat16)


def dot(left, right):
    return jnp.dot(left, right, preferred_element_type=jnp.float32)


def kernel(
    n_gx,
    conc, therm, veloc, table_h, logs_h, barriers_h, heats_h, kappas_h, ymat_h, emat_h, zmat_h,
    next_out,
    past, lev_a, lev_n, lev_c, vel, xhalo, xterm, state1, state2, state3, zhalo, ypack, yhalo,
    rate, local, result, qbuf, made, parts, near, dy, dz1, dz2, edge, kpack, vpack, nuk,
    ymat, emat, zmat, ymat_v, emat_v, zmat_v,
    table_s, logs, barriers, heats, kappas, table_v,
    vel_near, relay, hop_send, hop_recv, on_send, past_sem, ld_sem, vel_send, swap_send, arrive, x_send, x_recv, z_send, z_recv, y_send, y_recv,
    o_send, o_recv,
):
    gx, gy, gz = lax.axis_index("gx"), lax.axis_index("gy"), lax.axis_index("gz")
    period = max(n_gx // 8, 1)

    def half_of(at):
        return lax.rem(lax.div(at, period), 2)

    mirrored = half_of(gx)
    moves = lax.rem(gy + gz + mirrored, 2) == 1

    def x_beside(at):
        flips = half_of(at) != mirrored
        return {
            "gx": at,
            "gy": jnp.where(flips, 1 - gy, gy),
            "gz": jnp.where(flips, 1 - gz, gz),
        }

    right = x_beside(lax.rem(gx + 1, n_gx))
    left = x_beside(lax.rem(gx + n_gx - 1, n_gx))
    z_partner = {"gx": gx, "gy": 1 - gy, "gz": gz}
    y_partner = {"gx": gx, "gy": gy, "gz": 1 - gz}
    opposite = {"gx": gx, "gy": 1 - gy, "gz": 1 - gz}

    def remote(src, dst, send, recv, where):
        return pltpu.make_async_remote_copy(
            src_ref=src, dst_ref=dst, send_sem=send, recv_sem=recv,
            device_id=where, device_id_type=MESH,
        )

    past_loads = []
    for chunk, (begin, end) in enumerate(CHUNKS):
        stop = min(end, SPECIES)
        copies = [(conc.at[:, begin:stop], past.at[:, begin:stop])]
        if end == FIELDS:
            copies.append((therm, past.at[:, SPECIES]))
        past_loads.append([
            pltpu.make_async_copy(src, dst, past_sem.at[chunk, at])
            for at, (src, dst) in enumerate(copies)
        ])
    shared = ((table_h, table_v), (ymat_h, ymat_v), (emat_h, emat_v), (zmat_h, zmat_v), (table_h, table_s),
              (logs_h, logs), (barriers_h, barriers), (heats_h, heats), (kappas_h, kappas),
              (veloc, vel_near))
    loads = [
        pltpu.make_async_copy(src, dst, ld_sem.at[at]) for at, (src, dst) in enumerate(shared)
    ]
    for copy in [copy for copies in past_loads for copy in copies] + loads:
        copy.start()

    barrier = pltpu.get_barrier_semaphore()
    for where in (left, right, z_partner, y_partner, opposite):
        pl.semaphore_signal(barrier, inc=1, device_id=where, device_id_type=MESH)

    def moved(level, chunk):
        begin, end = CHUNKS[chunk]
        return past.at[level, begin:end], (lev_a, lev_n, lev_c)[level].at[begin:end]

    def swap(level, chunk):
        src, dst = moved(level, chunk)
        return remote(src, dst, swap_send.at[level, chunk], arrive.at[level, chunk], opposite)

    def hop(chunk):
        span = slice(*CHUNKS[chunk])
        return remote(
            past.at[2, span], relay.at[0, span], hop_send.at[chunk], hop_recv.at[0, chunk],
            z_partner,
        )

    def on(chunk):
        span = slice(*CHUNKS[chunk])
        return remote(
            relay.at[0, span], lev_c.at[span], on_send.at[0, chunk], arrive.at[2, chunk], y_partner
        )

    def own(level, chunk):
        src, dst = moved(level, chunk)
        return pltpu.make_async_copy(src, dst, arrive.at[level, chunk])

    def placed(level, chunk):
        src, dst = moved(level, chunk)
        pltpu.make_async_copy(dst, dst, arrive.at[level, chunk]).wait()

    vel_swap = remote(vel_near, vel, vel_send.at[0], vel_send.at[1], opposite)
    vel_own = pltpu.make_async_copy(vel_near, vel, vel_send.at[1])

    levels = (lev_a, lev_n, lev_c)

    def x_copies(level, chunk, source=None):
        begin, end = CHUNKS[chunk]
        src = (levels[level] if source is None else source).at[begin:end]
        return [
            remote(
                src, xhalo.at[level, side, begin:end],
                x_send.at[level, side, chunk], x_recv.at[level, side, chunk], where,
            )
            for side, where in ((0, right), (1, left))
        ]

    def delay(chunk):
        for copy in past_loads[chunk]:
            copy.wait()

        def one(field, carry):
            past[0, field] = 2.0 * past[1, field] - past[0, field]
            return carry

        lax.fori_loop(*CHUNKS[chunk], one, 0, unroll=2)

    def start(copies):
        for copy in copies:
            copy.start()

    stays = jnp.logical_not(moves)
    chunks = range(len(CHUNKS))

    for chunk in chunks:
        delay(chunk)
    loads[-1].wait()
    pl.semaphore_wait(barrier, 5)

    @pl.when(stays)
    def _():
        vel_own.start()
        for chunk in chunks:
            own(2, chunk).start()
        for chunk in chunks:
            start(x_copies(0, chunk, past.at[0]))

    @pl.when(moves)
    def _():
        for chunk in chunks:
            hop(chunk).start()
            swap(0, chunk).start()
        vel_swap.start()
        for chunk in chunks:
            swap(1, chunk).start()

    for load in loads[:-1]:
        load.wait()

    def place_of_mean(j, carry):
        for side in range(2):
            member = table_s[side, j]
            table_s[side, j] = jnp.where(member == SPECIES, FIELDS, member)
        return carry

    lax.fori_loop(0, REACT, place_of_mean, 0)
    for matrix, into in ((ymat_v, ymat), (emat_v, emat), (zmat_v, zmat)):
        into[...] = matrix[...].astype(jnp.bfloat16)

    filler = jnp.full((4, CY - REACT), 31.0, jnp.float32)
    members = jnp.concatenate([table_v[...].astype(jnp.float32), filler], axis=1)
    members = jnp.concatenate([members, jnp.zeros((12, CY), jnp.float32)], axis=0)
    column = lax.broadcasted_iota(jnp.int32, (CY, 2 * QROWS), 1)
    column = jnp.where(column >= QROWS, column - QROWS, column)
    reaction = lax.broadcasted_iota(jnp.int32, (CY, 2 * QROWS), 0)
    spread = jnp.where(lax.shift_right_logical(column, 3) == reaction, 1.0, 0.0)
    members = dot(members.astype(jnp.bfloat16), spread.astype(jnp.bfloat16))
    level_z = lax.broadcasted_iota(jnp.int32, (CZ, 2 * QROWS), 0)
    same_z = (lax.broadcasted_iota(jnp.int32, (CZ, 2 * QROWS), 1) & 7) == level_z
    for species in range(0, FIELDS, 2):
        both = []
        for at in (species, species + 1):
            total = jnp.zeros((1, 2 * QROWS), jnp.float32)
            if at < SPECIES:
                for which, sign in ((0, -1.0), (1, -1.0), (2, 1.0), (3, 1.0)):
                    total = total + jnp.where(members[which : which + 1] == at, sign, 0.0)
            both.append(jnp.where(same_z, total, 0.0))
        rows = slice(CZ * species, CZ * species + 2 * CZ)
        nuk[rows, :] = jnp.concatenate(both, axis=0).astype(jnp.bfloat16)
    filled = (REACT + 1) * CZ
    for begin in (filled, QROWS + filled):
        qbuf[begin : begin + QROWS - filled, :] = jnp.zeros((QROWS - filled, LANES), jnp.bfloat16)

    lane_block = lax.broadcasted_iota(jnp.int32, (CZ, CY), 1) // 8
    lane = lax.broadcasted_iota(jnp.int32, (CZ, CY), 1)
    at_edge = jnp.logical_or(lane < 4, lane >= CY - 4)
    for quad in range(QUADS):
        packed = jnp.zeros((CZ, CY), jnp.float32)
        for slab in range(min(QUAD, FIELDS - QUAD * quad)):
            packed = jnp.where(
                lane_block // CX == slab, kappas[0, QUAD * quad + slab], packed
            )
        kpack[quad] = packed * (1.0 / SECOND_SCALE)

    @pl.when(moves)
    def _():
        for chunk in chunks:
            placed(0, chunk)
            start(x_copies(0, chunk))

    def z_copy(k, state, chunk):
        begin, end = CHUNKS[chunk]
        return remote(
            state.at[begin:end], zhalo.at[k, begin:end], z_send.at[k, chunk], z_recv.at[k, chunk],
            z_partner,
        )

    def y_copy(k):
        return remote(ypack.at[k], yhalo.at[k], y_send.at[k], y_recv.at[k], y_partner)

    def pack(columns):
        packed = jnp.zeros((CZ, CY), jnp.float32)
        for at, value in enumerate(columns):
            packed = jnp.where(lane_block == at, pltpu.roll(value, (8 * at + 4) % CY, 1), packed)
        return packed

    def send_borders(k, state, chunk):
        z_copy(k, state, chunk).start()
        begin, end = CHUNKS[chunk]
        for first in range(begin, end, QUAD):
            fields = range(first, min(first + QUAD, end))
            ypack[k, first // QUAD] = pack([state[f, x] for f in fields for x in range(CX)])
        if end == FIELDS:
            y_copy(k).start()

    def reactions(state):
        total = state[0]
        for species in range(1, SPECIES):
            total = total + state[species]
        state[FIELDS] = total * (1.0 / SPECIES)
        inverse = 1.0 / state[SPECIES]

        def two(pair, carry):
            both = []
            for at in range(2):
                j = jnp.minimum(2 * pair + at, REACT - 1)
                first, second = table_s[0, j], table_s[1, j]
                speed = jnp.exp(logs[0, j] - barriers[0, j] * inverse)
                both.append(speed * state[first] * state[second])
            begin = pl.multiple_of(16 * pair, 16)
            for x in range(CX):
                high, low = split(jnp.concatenate([both[0][x], both[1][x]], axis=0))
                lanes = slice(CY * x, CY * x + CY)
                qbuf[pl.ds(begin, 16), lanes] = high
                qbuf[pl.ds(QROWS + begin, 16), lanes] = low
            return carry

        lax.fori_loop(0, (REACT + 1) // 2, two, 0, unroll=8)

    def in_parts(source, into):
        for f in range(0, FIELDS, 2):
            for x in range(CX):
                rows = slice(ROWS * x + CZ * f, ROWS * x + CZ * f + 16)
                value = jnp.concatenate([source[f, x], source[f + 1, x]], axis=0)
                into[rows, 0:CY], into[rows, CY:] = split(value)

    def transport(k, state, finish, done=None):
        made[...] = dot(nuk[...], qbuf[...]).reshape(FIELDS, CZ, LANES)
        in_parts(state, parts)
        for chunk in chunks:
            z_copy(k, state, chunk).wait_recv()
        dy[...] = dot(parts[...], ymat[...]).reshape(CX, FIELDS, CZ, 2 * CY)
        in_parts(zhalo.at[k], near)
        for first in (0, 4, 8, 12, 14):
            for x in range(0, CX, 2):
                sides = []
                for at in (x, x + 1):
                    rows = slice(ROWS * at + CZ * first, ROWS * at + CZ * (first + QUAD))
                    sides.append(jnp.concatenate(
                        [parts[rows, 0:CY], near[rows, 0:CY], parts[rows, CY:], near[rows, CY:]],
                        axis=0,
                    ))
                out = dot(zmat[...], jnp.concatenate(sides, axis=1))
                lanes = slice(CY * x, CY * x + 2 * CY)
                dz1[first : first + QUAD, :, lanes] = out[: QUAD * CZ].reshape(QUAD, CZ, 2 * CY)
                dz2[first : first + QUAD, :, lanes] = out[QUAD * CZ :].reshape(QUAD, CZ, 2 * CY)
        y_copy(k).wait_recv()
        value = jnp.concatenate(
            [yhalo[k].reshape(QUADS * CZ, CY), jnp.zeros((CZ, CY), jnp.float32)], axis=0
        )
        out = dot(jnp.concatenate(split(value), axis=1), emat[...])
        for quad in range(QUADS):
            part = out[CZ * quad : CZ * quad + CZ]
            edge[quad] = kpack[quad] * part[:, CY:] - vpack[...] * part[:, 0:CY]

        def one(f, x, packed, at, source):
            values = [state[f, q] for q in range(CX)]
            grad, curv = None, (3.0 * center_coeff) * values[x]
            for q in range(CX):
                if q != x:
                    first, second = weight(q - x)
                    curv = curv + second * values[q]
                    grad = first * values[q] if grad is None else grad + first * values[q]
            lanes = slice(CY * x, CY * x + CY)
            curv = curv + (1.0 / SECOND_SCALE) * (dy[x, f, :, CY:] + dz2[f, :, lanes])
            along = vel[0, x] * grad + vel[1, x] * dy[x, f, :, 0:CY] + vel[2, x] * dz1[f, :, lanes]
            border = pltpu.roll(packed, (CY - (8 * at + 4)) % CY, 1)
            source = source + jnp.where(at_edge, border, 0.0)
            finish(f, x, kappas[0, f] * curv - along + source)

        def quad_of_fields(quad, release, fields=QUAD):
            release = list(release)
            packed = edge[quad]
            for slab in range(fields):
                f = QUAD * quad + slab
                for x in range(CX):
                    at = slab * CX + x
                    if slab == 1 and fields == 2:
                        one(f, x, packed, at, release[x])
                        continue
                    source = made[f, :, CY * x : CY * x + CY]
                    release[x] = release[x] + heats[0, f] * source
                    one(f, x, packed, at, source)
            return tuple(release)

        release = (jnp.zeros((CZ, CY), jnp.float32),) * CX
        if done is None:
            release = lax.fori_loop(0, QUADS - 1, quad_of_fields, release)
            quad_of_fields(QUADS - 1, release, fields=2)
            return
        for chunk, (begin, end) in enumerate(CHUNKS):
            release = lax.fori_loop(begin // QUAD, end // QUAD, quad_of_fields, release)
            if end == FIELDS:
                quad_of_fields(QUADS - 1, release, fields=2)
            done(chunk)

    def x_halo(level, make, done):
        def one(f, carry):
            before = [xhalo[level, 0, f, q] for q in range(CX)]
            after = [xhalo[level, 1, f, q] for q in range(CX)]
            for x in range(CX):
                grad = curv = None
                for q in range(CX):
                    for value, distance in ((before[q], q - 4 - x), (after[q], q + 4 - x)):
                        first, second = weight(distance)
                        if second == 0.0:
                            continue
                        grad = first * value if grad is None else grad + first * value
                        curv = second * value if curv is None else curv + second * value
                make(f, x, kappas[0, f] * curv - vel[0, x] * grad)
            return carry

        for chunk in chunks:
            for copy in x_copies(level, chunk):
                copy.wait_recv()
            lax.fori_loop(*CHUNKS[chunk], one, 0, unroll=4 if chunk < 2 else 2)
            done(chunk)

    def keep(f, x, value):
        local[f, x] = value

    @pl.when(stays)
    def _():
        for chunk in chunks:
            hop(chunk).wait_recv()
            on(chunk).start()

    for chunk in chunks:
        placed(2, chunk)
        send_borders(0, lev_c, chunk)

    @pl.when(stays)
    def _():
        for level in (1, 2):
            for chunk in chunks:
                start(x_copies(level, chunk, past.at[level]))

    reactions(lev_c)

    @pl.when(moves)
    def _():
        placed(1, 0)
        start(x_copies(1, 0))


    vel_own.wait()
    for x in range(CX):
        vel[1, x] = vel[1, x] * (1.0 / FIRST_SCALE)
        vel[2, x] = vel[2, x] * (1.0 / FIRST_SCALE)
    vpack[...] = pack([vel[1, x] for x in range(CX)] * QUAD)
    transport(0, lev_c, keep)

    @pl.when(moves)
    def _():
        for chunk in chunks[1:]:
            placed(1, chunk)
            start(x_copies(1, chunk))
        for chunk in chunks:
            start(x_copies(2, chunk))

    def make(f, x, share):
        xterm[0, f, x] = share
        value = local[f, x] + share
        rate[f, x] = value
        state1[f, x] = lev_c[f, x] + time_step * value

    x_halo(0, make, lambda chunk: send_borders(1, state1, chunk))

    reactions(state1)
    transport(1, state1, keep)

    def make(f, x, share):
        xterm[1, f, x] = share
        value = local[f, x] + 2.0 * xterm[0, f, x] - share
        state2[f, x] = lev_c[f, x] + 0.5 * time_step * (rate[f, x] + value)

    x_halo(1, make, lambda chunk: send_borders(2, state2, chunk))

    reactions(state2)
    transport(2, state2, keep)

    def make(f, x, late):
        before = xterm[1, f, x]
        value = local[f, x] + 2.0 * late - before
        state3[f, x] = state2[f, x] + time_step * value
        rate[f, x] = value + 3.0 * late - 2.0 * before

    x_halo(2, make, lambda chunk: send_borders(3, state3, chunk))

    reactions(state3)

    def last(f, x, value):
        result[f, x] = state2[f, x] + 0.5 * time_step * (rate[f, x] + value)

    def outs(chunk):
        begin, end = CHUNKS[chunk]
        return result.at[begin:end], next_out.at[begin:end]

    def out_swap(chunk):
        src, dst = outs(chunk)
        where, recv = opposite, o_recv.at[chunk]
        if chunk in BESIDE:
            dst, where, recv = relay.at[1, slice(*CHUNKS[chunk])], z_partner, hop_recv.at[1, chunk]
        return remote(src, dst, o_send.at[chunk], recv, where)

    def out_on(chunk):
        span = slice(*CHUNKS[chunk])
        return remote(
            relay.at[1, span], next_out.at[span], on_send.at[1, chunk], o_recv.at[chunk], y_partner
        )

    def out_own(chunk):
        src, dst = outs(chunk)
        return pltpu.make_async_copy(src, dst, o_recv.at[chunk])

    def done(chunk):
        @pl.when(moves)
        def _():
            out_swap(chunk).start()

        @pl.when(stays)
        def _():
            out_own(chunk).start()

    transport(3, state3, last, done)

    @pl.when(stays)
    def _():
        for chunk in BESIDE:
            out_swap(chunk).wait_recv()
            out_on(chunk).start()

    for level in range(3):
        for chunk in chunks:
            for copy in x_copies(level, chunk):
                copy.wait_send()
    for k, state in enumerate((lev_c, state1, state2, state3)):
        for chunk in chunks:
            z_copy(k, state, chunk).wait_send()
        y_copy(k).wait_send()

    @pl.when(moves)
    def _():
        vel_swap.wait_send()
        for chunk in chunks:
            for copy in (swap(0, chunk), swap(1, chunk), hop(chunk), out_swap(chunk)):
                copy.wait_send()

    @pl.when(stays)
    def _():
        for chunk in chunks:
            on(chunk).wait_send()
        for chunk in BESIDE:
            out_on(chunk).wait_send()

    for chunk in chunks:
        out_own(chunk).wait()


def hand_out(next_ref, conc_out, therm_out, sem):
    copies = [
        pltpu.make_async_copy(next_ref.at[0:SPECIES], conc_out, sem.at[0]),
        pltpu.make_async_copy(next_ref.at[SPECIES], therm_out, sem.at[1]),
    ]
    for copy in copies:
        copy.start()
    for copy in copies:
        copy.wait()


def local(
    concentration_levels,
    thermal_levels,
    fluid_velocity,
    diffusivity,
    natural_logged_prefactors,
    energy_barrier_kelvin,
    enthalpy_yield_per_mole,
    stoichiometric_member_table,
):
    n_gx = lax.axis_size("gx")
    any_space = pl.BlockSpec(memory_space=pl.ANY)
    f32, bf16 = jnp.float32, jnp.bfloat16
    block = (FIELDS, CX, CZ, CY)
    wide = (FIELDS + 1, CX, CZ, CY)
    parts = len(CHUNKS)
    dma = pltpu.SemaphoreType.DMA
    scratch = [
        pltpu.VMEM((3,) + block, f32),
        pltpu.VMEM(block, f32),
        pltpu.VMEM(block, f32),
        pltpu.VMEM(wide, f32),
        pltpu.VMEM((3, CX, CZ, CY), f32),
        pltpu.VMEM((3, 2) + block, f32),
        pltpu.VMEM((2,) + block, f32),
        pltpu.VMEM(wide, f32),
        pltpu.VMEM(wide, f32),
        pltpu.VMEM(wide, f32),
        pltpu.VMEM((4,) + block, f32),
        pltpu.VMEM((4, QUADS, CZ, CY), f32),
        pltpu.VMEM((4, QUADS, CZ, CY), f32),
        pltpu.VMEM(block, f32),
        pltpu.VMEM(block, f32),
        pltpu.VMEM(block, f32),
        pltpu.VMEM((2 * QROWS, LANES), bf16),
        pltpu.VMEM((FIELDS, CZ, LANES), f32),
        pltpu.VMEM((CX * ROWS, 2 * CY), bf16),
        pltpu.VMEM((CX * ROWS, 2 * CY), bf16),
        pltpu.VMEM((CX, FIELDS, CZ, 2 * CY), f32),
        pltpu.VMEM((FIELDS, CZ, LANES), f32),
        pltpu.VMEM((FIELDS, CZ, LANES), f32),
        pltpu.VMEM((QUADS, CZ, CY), f32),
        pltpu.VMEM((QUADS, CZ, CY), f32),
        pltpu.VMEM((CZ, CY), f32),
        pltpu.VMEM((ROWS, 2 * QROWS), bf16),
        pltpu.VMEM((2 * CY, 2 * CY), bf16),
        pltpu.VMEM((2 * CY, 2 * CY), bf16),
        pltpu.VMEM((2 * QUAD * CZ, 4 * QUAD * CZ), bf16),
        pltpu.VMEM((2 * CY, 2 * CY), f32),
        pltpu.VMEM((2 * CY, 2 * CY), f32),
        pltpu.VMEM((2 * QUAD * CZ, 4 * QUAD * CZ), f32),
        pltpu.SMEM((4, REACT), jnp.int32),
        pltpu.SMEM((1, REACT), f32),
        pltpu.SMEM((1, REACT), f32),
        pltpu.SMEM((1, SPECIES), f32),
        pltpu.SMEM((1, FIELDS), f32),
        pltpu.VMEM((4, REACT), jnp.int32),
        pltpu.VMEM((3, CX, CZ, CY), f32),
        pltpu.VMEM((2,) + block, f32),
        dma((parts,)),
        dma((2, parts)),
        dma((2, parts)),
        dma((parts, 2)),
        dma((10,)),
        dma((2,)),
        dma((3, parts)),
        dma((3, parts)),
        dma((3, 2, parts)),
        dma((3, 2, parts)),
        dma((4, parts)),
        dma((4, parts)),
        dma((4,)),
        dma((4,)),
        dma((parts,)),
        dma((parts,)),
    ]
    stepped = pl.pallas_call(
        functools.partial(kernel, n_gx),
        out_shape=pltpu.VMEM(block, f32),
        in_specs=[any_space] * 11,
        out_specs=any_space,
        scratch_shapes=scratch,
        compiler_params=pltpu.CompilerParams(
            collective_id=0, has_side_effects=True, vmem_limit_bytes=40 * 1024 * 1024
        ),
    )(*[pltpu.with_memory_space_constraint(value, pltpu.HBM) for value in (
        concentration_levels,
        thermal_levels,
        fluid_velocity,
        stoichiometric_member_table,
        natural_logged_prefactors[None],
        energy_barrier_kelvin[None],
        enthalpy_yield_per_mole[None],
        diffusivity[None],
        jnp.asarray(y_matrix()),
        jnp.asarray(edge_matrix()),
        jnp.asarray(z_matrix()),
    )])
    return pl.pallas_call(
        hand_out,
        out_shape=(
            jax.ShapeDtypeStruct((SPECIES, CX, CZ, CY), f32),
            jax.ShapeDtypeStruct((CX, CZ, CY), f32),
        ),
        in_specs=[any_space],
        out_specs=(any_space, any_space),
        scratch_shapes=[dma((2,))],
        compiler_params=pltpu.CompilerParams(vmem_limit_bytes=8 * 1024 * 1024),
    )(stepped)


def solution(mesh):
    in_specs = (
        P(None, None, "gx", "gz", "gy"),
        P(None, "gx", "gz", "gy"),
        P(None, "gx", "gz", "gy"),
        P(),
        P(),
        P(),
        P(),
        P(),
    )
    out_specs = (P(None, "gx", "gz", "gy"), P("gx", "gz", "gy"))
    return jax.shard_map(local, mesh=mesh, in_specs=in_specs, out_specs=out_specs, check_vma=False)
```

```python
import functools

import jax
import jax.numpy as jnp
import numpy as np
from jax import lax
from jax.experimental import pallas as pl
from jax.experimental.pallas import tpu as pltpu
from jax.sharding import PartitionSpec as P

SPECIES = 17
FIELDS = 18
REACT = 73
CX = 4
CZ = 8
CY = 128
ROWS = FIELDS * CZ
LANES = CX * CY
QUAD = 4
QUADS = (FIELDS + QUAD - 1) // QUAD
QROWS = 640
CHUNKS = ((0, 8), (8, 16), (16, 18))
BESIDE = (1,)

time_step = 0.125
first_coeffs = (4.0 / 5.0, -1.0 / 5.0, 4.0 / 105.0, -1.0 / 280.0)
second_coeffs = (8.0 / 5.0, -1.0 / 5.0, 8.0 / 315.0, -1.0 / 560.0)
center_coeff = -205.0 / 72.0

MESH = pl.DeviceIdType.MESH


FIRST_SCALE = 840.0
SECOND_SCALE = 5040.0
first_scaled = (672.0, -168.0, 32.0, -3.0)
second_scaled = (8064.0, -1008.0, 128.0, -9.0)


def weight(distance):
    size = abs(distance)
    if size == 0 or size > 4:
        return 0.0, 0.0
    sign = 1.0 if distance > 0 else -1.0
    return sign * first_coeffs[size - 1], second_coeffs[size - 1]


def scaled(distance):
    size = abs(distance)
    if size == 0 or size > 4:
        return 0.0, 0.0
    sign = 1.0 if distance > 0 else -1.0
    return sign * first_scaled[size - 1], second_scaled[size - 1]


def y_matrix():
    matrix = np.zeros((CY, 2 * CY), np.float32)
    for out in range(CY):
        for at in range(CY):
            matrix[at, out], matrix[at, CY + out] = scaled(at - out)
    return np.concatenate([matrix, matrix])


def edge_matrix():
    matrix = np.zeros((CY, 2 * CY), np.float32)
    for base in range(0, CY, 8):
        for at in range(8):
            for out in range(8):
                if (at < 4) != (out < 4):
                    first, second = scaled(at - out)
                    matrix[base + at, base + out] = first
                    matrix[base + at, CY + base + out] = second
    return np.concatenate([matrix, matrix])


def z_matrix():
    half = QUAD * CZ
    matrix = np.zeros((2 * half, 2 * half), np.float32)
    for slab in range(QUAD):
        for out in range(CZ):
            for step in range(-4, 5):
                at = out + step
                column = slab * CZ + at % CZ + (0 if 0 <= at < CZ else half)
                first, second = scaled(step)
                matrix[slab * CZ + out, column] += first
                matrix[half + slab * CZ + out, column] += second
    return np.concatenate([matrix, matrix], axis=1)


def split(value):
    high = value.astype(jnp.bfloat16)
    return high, (value - high.astype(jnp.float32)).astype(jnp.bfloat16)


def dot(left, right):
    return jnp.dot(left, right, preferred_element_type=jnp.float32)


def kernel(
    n_gx,
    conc, therm, veloc, table_h, logs_h, barriers_h, heats_h, kappas_h, ymat_h, emat_h, zmat_h,
    next_out,
    past, lev_a, lev_n, lev_c, vel, xhalo, xterm, state1, state2, state3, zhalo, ypack, yhalo,
    rate, local, result, qbuf, made, parts, near, dy, dz1, dz2, edge, kpack, vpack, nuk,
    ymat, emat, zmat, ymat_v, emat_v, zmat_v,
    table_s, logs, barriers, heats, kappas, table_v,
    vel_near, relay, hop_send, hop_recv, on_send, past_sem, ld_sem, vel_send, swap_send, arrive, x_send, x_recv, z_send, z_recv, y_send, y_recv,
    o_send, o_recv,
):
    gx, gy, gz = lax.axis_index("gx"), lax.axis_index("gy"), lax.axis_index("gz")
    period = max(n_gx // 8, 1)

    def half_of(at):
        return lax.rem(lax.div(at, period), 2)

    mirrored = half_of(gx)
    moves = lax.rem(gy + gz + mirrored, 2) == 1

    def x_beside(at):
        flips = half_of(at) != mirrored
        return {
            "gx": at,
            "gy": jnp.where(flips, 1 - gy, gy),
            "gz": jnp.where(flips, 1 - gz, gz),
        }

    right = x_beside(lax.rem(gx + 1, n_gx))
    left = x_beside(lax.rem(gx + n_gx - 1, n_gx))
    z_partner = {"gx": gx, "gy": 1 - gy, "gz": gz}
    y_partner = {"gx": gx, "gy": gy, "gz": 1 - gz}
    opposite = {"gx": gx, "gy": 1 - gy, "gz": 1 - gz}

    def remote(src, dst, send, recv, where):
        return pltpu.make_async_remote_copy(
            src_ref=src, dst_ref=dst, send_sem=send, recv_sem=recv,
            device_id=where, device_id_type=MESH,
        )

    past_loads = []
    for chunk, (begin, end) in enumerate(CHUNKS):
        stop = min(end, SPECIES)
        copies = [(conc.at[:, begin:stop], past.at[:, begin:stop])]
        if end == FIELDS:
            copies.append((therm, past.at[:, SPECIES]))
        past_loads.append([
            pltpu.make_async_copy(src, dst, past_sem.at[chunk, at])
            for at, (src, dst) in enumerate(copies)
        ])
    shared = ((table_h, table_v), (ymat_h, ymat_v), (emat_h, emat_v), (zmat_h, zmat_v), (table_h, table_s),
              (logs_h, logs), (barriers_h, barriers), (heats_h, heats), (kappas_h, kappas),
              (veloc, vel_near))
    loads = [
        pltpu.make_async_copy(src, dst, ld_sem.at[at]) for at, (src, dst) in enumerate(shared)
    ]
    for copy in [copy for copies in past_loads for copy in copies] + loads:
        copy.start()

    barrier = pltpu.get_barrier_semaphore()
    for where in (left, right, z_partner, y_partner, opposite):
        pl.semaphore_signal(barrier, inc=1, device_id=where, device_id_type=MESH)

    def moved(level, chunk):
        begin, end = CHUNKS[chunk]
        return past.at[level, begin:end], (lev_a, lev_n, lev_c)[level].at[begin:end]

    def swap(level, chunk):
        src, dst = moved(level, chunk)
        return remote(src, dst, swap_send.at[level, chunk], arrive.at[level, chunk], opposite)

    def hop(chunk):
        span = slice(*CHUNKS[chunk])
        return remote(
            past.at[2, span], relay.at[0, span], hop_send.at[chunk], hop_recv.at[0, chunk],
            z_partner,
        )

    def on(chunk):
        span = slice(*CHUNKS[chunk])
        return remote(
            relay.at[0, span], lev_c.at[span], on_send.at[0, chunk], arrive.at[2, chunk], y_partner
        )

    def own(level, chunk):
        src, dst = moved(level, chunk)
        return pltpu.make_async_copy(src, dst, arrive.at[level, chunk])

    def placed(level, chunk):
        src, dst = moved(level, chunk)
        pltpu.make_async_copy(dst, dst, arrive.at[level, chunk]).wait()

    vel_swap = remote(vel_near, vel, vel_send.at[0], vel_send.at[1], opposite)
    vel_own = pltpu.make_async_copy(vel_near, vel, vel_send.at[1])

    levels = (lev_a, lev_n, lev_c)

    def x_copies(level, chunk, source=None):
        begin, end = CHUNKS[chunk]
        src = (levels[level] if source is None else source).at[begin:end]
        return [
            remote(
                src, xhalo.at[level, side, begin:end],
                x_send.at[level, side, chunk], x_recv.at[level, side, chunk], where,
            )
            for side, where in ((0, right), (1, left))
        ]

    def delay(chunk):
        for copy in past_loads[chunk]:
            copy.wait()

        def one(field, carry):
            past[0, field] = 2.0 * past[1, field] - past[0, field]
            return carry

        lax.fori_loop(*CHUNKS[chunk], one, 0, unroll=2)

    def start(copies):
        for copy in copies:
            copy.start()

    stays = jnp.logical_not(moves)
    chunks = range(len(CHUNKS))

    for chunk in chunks:
        delay(chunk)
    loads[-1].wait()
    pl.semaphore_wait(barrier, 5)

    @pl.when(stays)
    def _():
        vel_own.start()
        for chunk in chunks:
            own(2, chunk).start()
        for chunk in chunks:
            start(x_copies(0, chunk, past.at[0]))

    @pl.when(moves)
    def _():
        for chunk in chunks:
            hop(chunk).start()
            swap(0, chunk).start()
        vel_swap.start()
        for chunk in chunks:
            swap(1, chunk).start()

    @pl.when(stays)
    def _():
        for chunk in chunks:
            hop(chunk).wait_recv()
            on(chunk).start()

    for load in loads[:-1]:
        load.wait()

    def place_of_mean(j, carry):
        for side in range(2):
            member = table_s[side, j]
            table_s[side, j] = jnp.where(member == SPECIES, FIELDS, member)
        return carry

    lax.fori_loop(0, REACT, place_of_mean, 0)
    for matrix, into in ((ymat_v, ymat), (emat_v, emat), (zmat_v, zmat)):
        into[...] = matrix[...].astype(jnp.bfloat16)

    filler = jnp.full((4, CY - REACT), 31.0, jnp.float32)
    members = jnp.concatenate([table_v[...].astype(jnp.float32), filler], axis=1)
    members = jnp.concatenate([members, jnp.zeros((12, CY), jnp.float32)], axis=0)
    column = lax.broadcasted_iota(jnp.int32, (CY, 2 * QROWS), 1)
    column = jnp.where(column >= QROWS, column - QROWS, column)
    reaction = lax.broadcasted_iota(jnp.int32, (CY, 2 * QROWS), 0)
    spread = jnp.where(lax.shift_right_logical(column, 3) == reaction, 1.0, 0.0)
    members = dot(members.astype(jnp.bfloat16), spread.astype(jnp.bfloat16))
    level_z = lax.broadcasted_iota(jnp.int32, (CZ, 2 * QROWS), 0)
    same_z = (lax.broadcasted_iota(jnp.int32, (CZ, 2 * QROWS), 1) & 7) == level_z
    for species in range(0, FIELDS, 2):
        both = []
        for at in (species, species + 1):
            total = jnp.zeros((1, 2 * QROWS), jnp.float32)
            if at < SPECIES:
                for which, sign in ((0, -1.0), (1, -1.0), (2, 1.0), (3, 1.0)):
                    total = total + jnp.where(members[which : which + 1] == at, sign, 0.0)
            both.append(jnp.where(same_z, total, 0.0))
        rows = slice(CZ * species, CZ * species + 2 * CZ)
        nuk[rows, :] = jnp.concatenate(both, axis=0).astype(jnp.bfloat16)
    filled = (REACT + 1) * CZ
    for begin in (filled, QROWS + filled):
        qbuf[begin : begin + QROWS - filled, :] = jnp.zeros((QROWS - filled, LANES), jnp.bfloat16)

    lane_block = lax.broadcasted_iota(jnp.int32, (CZ, CY), 1) // 8
    lane = lax.broadcasted_iota(jnp.int32, (CZ, CY), 1)
    at_edge = jnp.logical_or(lane < 4, lane >= CY - 4)
    for quad in range(QUADS):
        packed = jnp.zeros((CZ, CY), jnp.float32)
        for slab in range(min(QUAD, FIELDS - QUAD * quad)):
            packed = jnp.where(
                lane_block // CX == slab, kappas[0, QUAD * quad + slab], packed
            )
        kpack[quad] = packed * (1.0 / SECOND_SCALE)

    @pl.when(moves)
    def _():
        for chunk in chunks:
            placed(0, chunk)
            start(x_copies(0, chunk))

    def z_copy(k, state, chunk):
        begin, end = CHUNKS[chunk]
        return remote(
            state.at[begin:end], zhalo.at[k, begin:end], z_send.at[k, chunk], z_recv.at[k, chunk],
            z_partner,
        )

    def y_copy(k):
        return remote(ypack.at[k], yhalo.at[k], y_send.at[k], y_recv.at[k], y_partner)

    def pack(columns):
        packed = jnp.zeros((CZ, CY), jnp.float32)
        for at, value in enumerate(columns):
            packed = jnp.where(lane_block == at, pltpu.roll(value, (8 * at + 4) % CY, 1), packed)
        return packed

    def send_borders(k, state, chunk):
        z_copy(k, state, chunk).start()
        begin, end = CHUNKS[chunk]
        for first in range(begin, end, QUAD):
            fields = range(first, min(first + QUAD, end))
            ypack[k, first // QUAD] = pack([state[f, x] for f in fields for x in range(CX)])
        if end == FIELDS:
            y_copy(k).start()

    def reactions(state):
        total = state[0]
        for species in range(1, SPECIES):
            total = total + state[species]
        state[FIELDS] = total * (1.0 / SPECIES)
        inverse = 1.0 / state[SPECIES]

        def two(pair, carry):
            both = []
            for at in range(2):
                j = jnp.minimum(2 * pair + at, REACT - 1)
                first, second = table_s[0, j], table_s[1, j]
                speed = jnp.exp(logs[0, j] - barriers[0, j] * inverse)
                both.append(speed * state[first] * state[second])
            begin = pl.multiple_of(16 * pair, 16)
            for x in range(CX):
                high, low = split(jnp.concatenate([both[0][x], both[1][x]], axis=0))
                lanes = slice(CY * x, CY * x + CY)
                qbuf[pl.ds(begin, 16), lanes] = high
                qbuf[pl.ds(QROWS + begin, 16), lanes] = low
            return carry

        lax.fori_loop(0, (REACT + 1) // 2, two, 0, unroll=4)

    def in_parts(source, into):
        for f in range(0, FIELDS, 2):
            for x in range(CX):
                rows = slice(ROWS * x + CZ * f, ROWS * x + CZ * f + 16)
                value = jnp.concatenate([source[f, x], source[f + 1, x]], axis=0)
                into[rows, 0:CY], into[rows, CY:] = split(value)

    def transport(k, state, finish, done=None):
        made[...] = dot(nuk[...], qbuf[...]).reshape(FIELDS, CZ, LANES)
        in_parts(state, parts)
        for chunk in chunks:
            z_copy(k, state, chunk).wait_recv()
        dy[...] = dot(parts[...], ymat[...]).reshape(CX, FIELDS, CZ, 2 * CY)
        in_parts(zhalo.at[k], near)
        for first in (0, 4, 8, 12, 14):
            for x in range(0, CX, 2):
                sides = []
                for at in (x, x + 1):
                    rows = slice(ROWS * at + CZ * first, ROWS * at + CZ * (first + QUAD))
                    sides.append(jnp.concatenate(
                        [parts[rows, 0:CY], near[rows, 0:CY], parts[rows, CY:], near[rows, CY:]],
                        axis=0,
                    ))
                out = dot(zmat[...], jnp.concatenate(sides, axis=1))
                lanes = slice(CY * x, CY * x + 2 * CY)
                dz1[first : first + QUAD, :, lanes] = out[: QUAD * CZ].reshape(QUAD, CZ, 2 * CY)
                dz2[first : first + QUAD, :, lanes] = out[QUAD * CZ :].reshape(QUAD, CZ, 2 * CY)
        y_copy(k).wait_recv()
        value = jnp.concatenate(
            [yhalo[k].reshape(QUADS * CZ, CY), jnp.zeros((CZ, CY), jnp.float32)], axis=0
        )
        out = dot(jnp.concatenate(split(value), axis=1), emat[...])
        for quad in range(QUADS):
            part = out[CZ * quad : CZ * quad + CZ]
            edge[quad] = kpack[quad] * part[:, CY:] - vpack[...] * part[:, 0:CY]

        def one(f, x, packed, at, source):
            values = [state[f, q] for q in range(CX)]
            grad, curv = None, (3.0 * center_coeff) * values[x]
            for q in range(CX):
                if q != x:
                    first, second = weight(q - x)
                    curv = curv + second * values[q]
                    grad = first * values[q] if grad is None else grad + first * values[q]
            lanes = slice(CY * x, CY * x + CY)
            curv = curv + (1.0 / SECOND_SCALE) * (dy[x, f, :, CY:] + dz2[f, :, lanes])
            along = vel[0, x] * grad + vel[1, x] * dy[x, f, :, 0:CY] + vel[2, x] * dz1[f, :, lanes]
            border = pltpu.roll(packed, (CY - (8 * at + 4)) % CY, 1)
            source = source + jnp.where(at_edge, border, 0.0)
            finish(f, x, kappas[0, f] * curv - along + source)

        def quad_of_fields(quad, release, fields=QUAD):
            release = list(release)
            packed = edge[quad]
            for slab in range(fields):
                f = QUAD * quad + slab
                for x in range(CX):
                    at = slab * CX + x
                    if slab == 1 and fields == 2:
                        one(f, x, packed, at, release[x])
                        continue
                    source = made[f, :, CY * x : CY * x + CY]
                    release[x] = release[x] + heats[0, f] * source
                    one(f, x, packed, at, source)
            return tuple(release)

        release = (jnp.zeros((CZ, CY), jnp.float32),) * CX
        if done is None:
            release = lax.fori_loop(0, QUADS - 1, quad_of_fields, release)
            quad_of_fields(QUADS - 1, release, fields=2)
            return
        for chunk, (begin, end) in enumerate(CHUNKS):
            release = lax.fori_loop(begin // QUAD, end // QUAD, quad_of_fields, release)
            if end == FIELDS:
                quad_of_fields(QUADS - 1, release, fields=2)
            done(chunk)

    def x_halo(level, make, done):
        def one(f, carry):
            before = [xhalo[level, 0, f, q] for q in range(CX)]
            after = [xhalo[level, 1, f, q] for q in range(CX)]
            for x in range(CX):
                grad = curv = None
                for q in range(CX):
                    for value, distance in ((before[q], q - 4 - x), (after[q], q + 4 - x)):
                        first, second = weight(distance)
                        if second == 0.0:
                            continue
                        grad = first * value if grad is None else grad + first * value
                        curv = second * value if curv is None else curv + second * value
                make(f, x, kappas[0, f] * curv - vel[0, x] * grad)
            return carry

        for chunk in chunks:
            for copy in x_copies(level, chunk):
                copy.wait_recv()
            lax.fori_loop(*CHUNKS[chunk], one, 0, unroll=4 if chunk < 2 else 2)
            done(chunk)

    def keep(f, x, value):
        local[f, x] = value

    for chunk in chunks:
        placed(2, chunk)
        send_borders(0, lev_c, chunk)

    @pl.when(stays)
    def _():
        for level in (1, 2):
            for chunk in chunks:
                start(x_copies(level, chunk, past.at[level]))

    reactions(lev_c)

    @pl.when(moves)
    def _():
        placed(1, 0)
        start(x_copies(1, 0))


    vel_own.wait()
    for x in range(CX):
        vel[1, x] = vel[1, x] * (1.0 / FIRST_SCALE)
        vel[2, x] = vel[2, x] * (1.0 / FIRST_SCALE)
    vpack[...] = pack([vel[1, x] for x in range(CX)] * QUAD)
    transport(0, lev_c, keep)

    @pl.when(moves)
    def _():
        for chunk in chunks[1:]:
            placed(1, chunk)
            start(x_copies(1, chunk))
        for chunk in chunks:
            start(x_copies(2, chunk))

    def make(f, x, share):
        xterm[0, f, x] = share
        value = local[f, x] + share
        rate[f, x] = value
        state1[f, x] = lev_c[f, x] + time_step * value

    x_halo(0, make, lambda chunk: send_borders(1, state1, chunk))

    reactions(state1)
    transport(1, state1, keep)

    def make(f, x, share):
        xterm[1, f, x] = share
        value = local[f, x] + 2.0 * xterm[0, f, x] - share
        state2[f, x] = lev_c[f, x] + 0.5 * time_step * (rate[f, x] + value)

    x_halo(1, make, lambda chunk: send_borders(2, state2, chunk))

    reactions(state2)
    transport(2, state2, keep)

    def make(f, x, late):
        before = xterm[1, f, x]
        value = local[f, x] + 2.0 * late - before
        state3[f, x] = state2[f, x] + time_step * value
        rate[f, x] = value + 3.0 * late - 2.0 * before

    x_halo(2, make, lambda chunk: send_borders(3, state3, chunk))

    reactions(state3)

    def last(f, x, value):
        result[f, x] = state2[f, x] + 0.5 * time_step * (rate[f, x] + value)

    def outs(chunk):
        begin, end = CHUNKS[chunk]
        return result.at[begin:end], next_out.at[begin:end]

    def out_swap(chunk):
        src, dst = outs(chunk)
        where, recv = opposite, o_recv.at[chunk]
        if chunk in BESIDE:
            dst, where, recv = relay.at[1, slice(*CHUNKS[chunk])], z_partner, hop_recv.at[1, chunk]
        return remote(src, dst, o_send.at[chunk], recv, where)

    def out_on(chunk):
        span = slice(*CHUNKS[chunk])
        return remote(
            relay.at[1, span], next_out.at[span], on_send.at[1, chunk], o_recv.at[chunk], y_partner
        )

    def out_own(chunk):
        src, dst = outs(chunk)
        return pltpu.make_async_copy(src, dst, o_recv.at[chunk])

    def done(chunk):
        @pl.when(moves)
        def _():
            out_swap(chunk).start()

        @pl.when(stays)
        def _():
            out_own(chunk).start()

    transport(3, state3, last, done)

    @pl.when(stays)
    def _():
        for chunk in BESIDE:
            out_swap(chunk).wait_recv()
            out_on(chunk).start()

    for level in range(3):
        for chunk in chunks:
            for copy in x_copies(level, chunk):
                copy.wait_send()
    for k, state in enumerate((lev_c, state1, state2, state3)):
        for chunk in chunks:
            z_copy(k, state, chunk).wait_send()
        y_copy(k).wait_send()

    @pl.when(moves)
    def _():
        vel_swap.wait_send()
        for chunk in chunks:
            for copy in (swap(0, chunk), swap(1, chunk), hop(chunk), out_swap(chunk)):
                copy.wait_send()

    @pl.when(stays)
    def _():
        for chunk in chunks:
            on(chunk).wait_send()
        for chunk in BESIDE:
            out_on(chunk).wait_send()

    for chunk in chunks:
        out_own(chunk).wait()


def hand_out(next_ref, conc_out, therm_out, sem):
    copies = [
        pltpu.make_async_copy(next_ref.at[0:SPECIES], conc_out, sem.at[0]),
        pltpu.make_async_copy(next_ref.at[SPECIES], therm_out, sem.at[1]),
    ]
    for copy in copies:
        copy.start()
    for copy in copies:
        copy.wait()


def local(
    concentration_levels,
    thermal_levels,
    fluid_velocity,
    diffusivity,
    natural_logged_prefactors,
    energy_barrier_kelvin,
    enthalpy_yield_per_mole,
    stoichiometric_member_table,
):
    n_gx = lax.axis_size("gx")
    any_space = pl.BlockSpec(memory_space=pl.ANY)
    f32, bf16 = jnp.float32, jnp.bfloat16
    block = (FIELDS, CX, CZ, CY)
    wide = (FIELDS + 1, CX, CZ, CY)
    parts = len(CHUNKS)
    dma = pltpu.SemaphoreType.DMA
    scratch = [
        pltpu.VMEM((3,) + block, f32),
        pltpu.VMEM(block, f32),
        pltpu.VMEM(block, f32),
        pltpu.VMEM(wide, f32),
        pltpu.VMEM((3, CX, CZ, CY), f32),
        pltpu.VMEM((3, 2) + block, f32),
        pltpu.VMEM((2,) + block, f32),
        pltpu.VMEM(wide, f32),
        pltpu.VMEM(wide, f32),
        pltpu.VMEM(wide, f32),
        pltpu.VMEM((4,) + block, f32),
        pltpu.VMEM((4, QUADS, CZ, CY), f32),
        pltpu.VMEM((4, QUADS, CZ, CY), f32),
        pltpu.VMEM(block, f32),
        pltpu.VMEM(block, f32),
        pltpu.VMEM(block, f32),
        pltpu.VMEM((2 * QROWS, LANES), bf16),
        pltpu.VMEM((FIELDS, CZ, LANES), f32),
        pltpu.VMEM((CX * ROWS, 2 * CY), bf16),
        pltpu.VMEM((CX * ROWS, 2 * CY), bf16),
        pltpu.VMEM((CX, FIELDS, CZ, 2 * CY), f32),
        pltpu.VMEM((FIELDS, CZ, LANES), f32),
        pltpu.VMEM((FIELDS, CZ, LANES), f32),
        pltpu.VMEM((QUADS, CZ, CY), f32),
        pltpu.VMEM((QUADS, CZ, CY), f32),
        pltpu.VMEM((CZ, CY), f32),
        pltpu.VMEM((ROWS, 2 * QROWS), bf16),
        pltpu.VMEM((2 * CY, 2 * CY), bf16),
        pltpu.VMEM((2 * CY, 2 * CY), bf16),
        pltpu.VMEM((2 * QUAD * CZ, 4 * QUAD * CZ), bf16),
        pltpu.VMEM((2 * CY, 2 * CY), f32),
        pltpu.VMEM((2 * CY, 2 * CY), f32),
        pltpu.VMEM((2 * QUAD * CZ, 4 * QUAD * CZ), f32),
        pltpu.SMEM((4, REACT), jnp.int32),
        pltpu.SMEM((1, REACT), f32),
        pltpu.SMEM((1, REACT), f32),
        pltpu.SMEM((1, SPECIES), f32),
        pltpu.SMEM((1, FIELDS), f32),
        pltpu.VMEM((4, REACT), jnp.int32),
        pltpu.VMEM((3, CX, CZ, CY), f32),
        pltpu.VMEM((2,) + block, f32),
        dma((parts,)),
        dma((2, parts)),
        dma((2, parts)),
        dma((parts, 2)),
        dma((10,)),
        dma((2,)),
        dma((3, parts)),
        dma((3, parts)),
        dma((3, 2, parts)),
        dma((3, 2, parts)),
        dma((4, parts)),
        dma((4, parts)),
        dma((4,)),
        dma((4,)),
        dma((parts,)),
        dma((parts,)),
    ]
    stepped = pl.pallas_call(
        functools.partial(kernel, n_gx),
        out_shape=pltpu.VMEM(block, f32),
        in_specs=[any_space] * 11,
        out_specs=any_space,
        scratch_shapes=scratch,
        compiler_params=pltpu.CompilerParams(
            collective_id=0, has_side_effects=True, vmem_limit_bytes=40 * 1024 * 1024
        ),
    )(*[pltpu.with_memory_space_constraint(value, pltpu.HBM) for value in (
        concentration_levels,
        thermal_levels,
        fluid_velocity,
        stoichiometric_member_table,
        natural_logged_prefactors[None],
        energy_barrier_kelvin[None],
        enthalpy_yield_per_mole[None],
        diffusivity[None],
        jnp.asarray(y_matrix()),
        jnp.asarray(edge_matrix()),
        jnp.asarray(z_matrix()),
    )])
    return pl.pallas_call(
        hand_out,
        out_shape=(
            jax.ShapeDtypeStruct((SPECIES, CX, CZ, CY), f32),
            jax.ShapeDtypeStruct((CX, CZ, CY), f32),
        ),
        in_specs=[any_space],
        out_specs=(any_space, any_space),
        scratch_shapes=[dma((2,))],
        compiler_params=pltpu.CompilerParams(vmem_limit_bytes=8 * 1024 * 1024),
    )(stepped)


def solution(mesh):
    in_specs = (
        P(None, None, "gx", "gz", "gy"),
        P(None, "gx", "gz", "gy"),
        P(None, "gx", "gz", "gy"),
        P(),
        P(),
        P(),
        P(),
        P(),
    )
    out_specs = (P(None, "gx", "gz", "gy"), P("gx", "gz", "gy"))
    return jax.shard_map(local, mesh=mesh, in_specs=in_specs, out_specs=out_specs, check_vma=False)
```
